512 devices in a mesh: neuron: 16 (over z), tm: 32 (over y, x, core).
Axes of the slice: x: 4, y: 4, z: 16, core: 2. Of those that a mesh axis runs over, the one named last changes fastest.
Arguments:
- spikes: int32 [65536, 8192], P('neuron', 'tm'), may hold values from 0 to 7
- read_weight: bfloat16 [65536, 256], P('neuron')
- in_proj: bfloat16 [256, 2048], P(None, 'neuron'), may hold values from -0.375 to 0.375
- decay_rate: float32 [2048], P('neuron'), may hold values from 1.2207031e-05 to 0.0333333333
- gate: float32 [8192], P('tm'), may hold values from 0.65 to 1
- out_fwd: bfloat16 [2048, 256], P('neuron'), may hold values from -0.125 to 0.125
- out_bwd: bfloat16 [2048, 256], P('neuron'), may hold values from -0.125 to 0.125
Outputs:
- latent: bfloat16 [8192, 256], P('tm')
- nll: float32 [65536], P('neuron')
The draws below stay inside these ranges and needn't reach their ends.
All inputs are finite; a program needn't handle non-finite values.
Results may differ from the reference program's by a relative error of at most 0.011.
Values may be sent and summed in bfloat16 or wider, within the bound.
No kernel may reach another device: no remote copies, remote signals or barrier semaphores. Data moves between devices by JAX's collectives and lax.ppermute only.
A program may use at most 64 MiB of HBM per device.

```python
import jax
import jax.numpy as jnp
from jax import lax

NEUR_DEV = 4096
CH = 256
NEURONS = 65536
BINS = 8192
MODES = 2048


def draw_spikes(key, part):
    key = jax.random.fold_in(key, 11)
    first, second = jax.random.split(key)
    counted = jax.random.randint(first, (NEURONS, BINS), 0, 8)
    keeper = jax.random.randint(second, (NEURONS, BINS), 0, 8)
    level = 2 + 6 * jnp.arange(BINS, dtype=jnp.int32) // BINS
    return jnp.where(keeper < level[None, :], counted, 0).astype(jnp.int32)


def draw_read_weight(key, part):
    key = jax.random.fold_in(key, 13)
    values = jax.random.normal(key, (NEURONS, CH), jnp.float32) * CH ** (-0.5)
    values = values - jnp.mean(values, axis=0, keepdims=True)
    return values.astype(jnp.bfloat16)


def draw_decay_rate(key, part):
    key = jax.random.fold_in(key, 17)
    first, second = jax.random.split(key)
    spread = jax.random.uniform(first, (MODES,), jnp.float32)
    picker = jax.random.uniform(second, (MODES,), jnp.float32)
    quick = jnp.exp(jnp.log(1.0 / 50.0) + spread * jnp.log(50.0 / 30.0))
    slow = jnp.exp(jnp.log(0.1 / BINS) + spread * jnp.log(10.0))
    rate = jnp.where(picker < 0.5, quick, slow)
    return rate.astype(jnp.float32)


def draw_gate(key, part):
    key = jax.random.fold_in(key, 19)
    first, second, third = jax.random.split(key, 3)
    base = 1.0 - 0.1 / BINS * jax.random.uniform(first, (BINS,), jnp.float32)
    places = jax.random.randint(second, (3,), 0, BINS)
    drops = 0.65 + 0.15 * jax.random.uniform(third, (3,), jnp.float32)
    return base.at[places].set(drops).astype(jnp.float32)


def steps_of(key, shape, cuts, low, top_value):
    loudness = 1.0
    for position, shards_of in cuts:
        heights = jax.random.uniform(jax.random.fold_in(jax.random.fold_in(key, 6), position), (shards_of,), jnp.float32, low / len(cuts), top_value / len(cuts))
        loudness = loudness * jnp.repeat(jnp.exp(heights), shape[position] // shards_of).reshape((-1,) + (1,) * (len(shape) - 1 - position))
    return loudness


def normal_values(key, dims, width, bound, cuts=(), kind=jnp.bfloat16):
    drawn = width * jax.random.normal(key, dims, jnp.float32)
    if cuts:
        drawn = drawn * steps_of(key, dims, cuts, -0.22, 0.18)
    return jnp.clip(drawn, -bound, bound).astype(kind)


def setup_inputs(seed: int = 0) -> dict:
    seeds = jax.random.split(jax.random.key(seed), 8)
    spikes = draw_spikes(jax.random.fold_in(seeds[7], 71), 0)
    read_weight = draw_read_weight(jax.random.fold_in(seeds[7], 71), 0)
    in_proj = normal_values(seeds[2], (CH, MODES), CH ** -0.5, 0.375, ((1, 16),))
    decay_rate = draw_decay_rate(jax.random.fold_in(seeds[7], 71), 0)
    gate = draw_gate(jax.random.fold_in(seeds[7], 71), 0)
    out_fwd = normal_values(seeds[5], (MODES, CH), MODES ** -0.5, 0.125, ((0, 16),))
    out_bwd = normal_values(seeds[6], (MODES, CH), MODES ** -0.5, 0.125, ((0, 16),))
    return {"spikes": spikes, "read_weight": read_weight, "in_proj": in_proj, "decay_rate": decay_rate, "gate": gate, "out_fwd": out_fwd, "out_bwd": out_bwd}


def advance(state, pair):
    factor, push = pair
    state = factor * state + push
    return (state, state)

def reference(spikes, read_weight, in_proj, decay_rate, gate, out_fwd, out_bwd):
    counts = spikes.astype(jnp.bfloat16)
    readin = lax.dot_general(counts, read_weight, (((0,), (0,)), ((), ())), preferred_element_type=jnp.float32)
    power = lax.optimization_barrier(jnp.mean(readin * readin, axis=-1, keepdims=True)) + 1e-05
    normed = (readin * lax.rsqrt(power)).astype(jnp.bfloat16)
    scale_in = jnp.sqrt(-jnp.expm1(-2.0 * decay_rate))
    drive = jnp.dot(normed, in_proj, preferred_element_type=jnp.float32) * scale_in[None, :]
    step = jnp.exp(-decay_rate)[None, :] * gate[:, None]
    start = jnp.zeros((drive.shape[1],), jnp.float32)
    _, forward = lax.scan(advance, start, (step, drive))
    _, backward = lax.scan(advance, start, (step, drive), reverse=True)
    mixed = jnp.dot(forward.astype(jnp.bfloat16), out_fwd, preferred_element_type=jnp.float32)
    mixed = mixed + jnp.dot(backward.astype(jnp.bfloat16), out_bwd, preferred_element_type=jnp.float32)
    latent = (normed.astype(jnp.float32) + mixed).astype(jnp.bfloat16)
    blocks = NEURONS // NEUR_DEV
    weight_blocks = read_weight.reshape(blocks, NEUR_DEV, read_weight.shape[1])
    spike_blocks = spikes.reshape(blocks, NEUR_DEV, spikes.shape[1])

    def block_nll(pair):
        weights, counted = pair
        log_rate = lax.dot_general(weights, latent, (((1,), (1,)), ((), ())), preferred_element_type=jnp.float32)
        terms = jnp.exp(log_rate) - counted.astype(jnp.float32) * log_rate
        return lax.optimization_barrier(jnp.sum(terms, axis=1)) / spikes.shape[1]
    nll = lax.map(block_nll, (weight_blocks, spike_blocks)).reshape(-1)
    return (latent, nll)
```

```python
import jax
import jax.numpy as jnp
from jax import lax
from jax.sharding import PartitionSpec as P

F32 = jnp.float32
BF16 = jnp.bfloat16
EXACT = lax.Precision.HIGHEST


def sum_rows(part, axis):
    count = lax.axis_size(axis)
    blocks = part.astype(BF16).reshape(count, part.shape[0] // count, part.shape[1])
    mine = lax.all_to_all(blocks, axis, 0, 0)
    return jnp.sum(mine.astype(F32), axis=0)


def body(spikes, read_weight, in_proj, decay_rate, gate, out_fwd, out_bwd):
    bins = spikes.shape[1]
    blocks = lax.axis_size("tm")
    place = lax.axis_index("tm")
    log_gate = jnp.log(gate)
    row = lax.broadcasted_iota(jnp.int32, (bins, bins), 0)
    col = lax.broadcasted_iota(jnp.int32, (bins, bins), 1)
    upto = jnp.sum(jnp.where(col <= row, log_gate[None, :], 0.0), axis=1)
    before = upto - log_gate
    upto_t = jnp.sum(jnp.where(row <= col, log_gate[:, None], 0.0), axis=0)
    before_t = upto_t - log_gate
    mix_fwd = jnp.where(col <= row, jnp.exp(jnp.minimum(upto[:, None] - upto_t[None, :], 0.0)), 0.0)
    mix_bwd = jnp.where(col >= row, jnp.exp(jnp.minimum(before_t[None, :] - before[:, None], 0.0)), 0.0)
    time = (lax.broadcasted_iota(jnp.int32, (bins, 1), 0) - bins // 2).astype(F32)
    grow = jnp.exp(time * decay_rate[None, :])
    shrink = jnp.exp(-time * decay_rate[None, :])
    first = jnp.arange(bins, dtype=jnp.int32).astype(F32)[:, None]
    cum_fwd = jnp.exp(upto[:, None] - (first + 1.0) * decay_rate[None, :])
    cum_bwd = jnp.exp((upto[-1] - before)[:, None] - (bins - first) * decay_rate[None, :])
    scale_in = jnp.sqrt(-jnp.expm1(-2.0 * decay_rate))

    counts = spikes.astype(BF16)
    partial_sum = lax.dot_general(
        counts, read_weight, (((0,), (0,)), ((), ())), preferred_element_type=F32
    )
    rows = sum_rows(partial_sum, "neuron")
    power = jnp.mean(rows * rows, axis=-1, keepdims=True) + 1e-05
    normed_rows = (rows * lax.rsqrt(power)).astype(BF16)
    normed = lax.all_gather(normed_rows, "neuron", tiled=True)

    drive = jnp.dot(normed, in_proj, preferred_element_type=F32) * scale_in[None, :]
    state_fwd = jnp.dot(mix_fwd, drive * grow, precision=EXACT) * shrink
    state_bwd = jnp.dot(mix_bwd, drive * shrink, precision=EXACT) * grow
    sent = jnp.stack([state_fwd[-1], state_bwd[0], jnp.broadcast_to(upto[-1], decay_rate.shape)])
    got = lax.all_gather(sent, "tm")
    loss = got[:, 2, :]
    order = jnp.arange(blocks, dtype=jnp.int32)[:, None]
    earlier = (order >= order.T).astype(F32)
    span = jnp.sum(earlier[:, :, None] * loss[None, :, :], axis=1)
    span_before = span - loss
    at_fwd = jnp.sum(jnp.where(order == place, span_before, 0.0), axis=0)
    at_bwd = jnp.sum(jnp.where(order == place, span, 0.0), axis=0)
    gap_fwd = ((place - 1 - order) * bins).astype(F32) * decay_rate[None, :]
    gap_bwd = ((order - 1 - place) * bins).astype(F32) * decay_rate[None, :]
    weight_fwd = jnp.where(order < place, jnp.exp(jnp.minimum(at_fwd[None, :] - span - gap_fwd, 0.0)), 0.0)
    weight_bwd = jnp.where(order > place, jnp.exp(jnp.minimum(span_before - at_bwd[None, :] - gap_bwd, 0.0)), 0.0)
    enter_fwd = jnp.sum(weight_fwd * got[:, 0, :], axis=0)
    enter_bwd = jnp.sum(weight_bwd * got[:, 1, :], axis=0)
    forward = state_fwd + cum_fwd * enter_fwd[None, :]
    backward = state_bwd + cum_bwd * enter_bwd[None, :]
    mixed_part = jnp.dot(forward.astype(BF16), out_fwd, preferred_element_type=F32)
    mixed_part = mixed_part + jnp.dot(backward.astype(BF16), out_bwd, preferred_element_type=F32)
    mixed_rows = sum_rows(mixed_part, "neuron")
    latent_rows = (normed_rows.astype(F32) + mixed_rows).astype(BF16)
    latent = lax.all_gather(latent_rows, "neuron", tiled=True)

    log_rate = lax.dot_general(
        read_weight, latent, (((1,), (1,)), ((), ())), preferred_element_type=F32
    )
    terms = jnp.exp(log_rate) - spikes.astype(F32) * log_rate
    part = jnp.sum(terms, axis=1).reshape(-1, 128)
    total = jnp.sum(lax.all_gather(part, "tm"), axis=0).reshape(-1)
    nll = total / (bins * blocks)
    return (latent, nll)


def solution(mesh):
    return jax.shard_map(
        body,
        mesh=mesh,
        in_specs=(
            P("neuron", "tm"),
            P("neuron", None),
            P(None, "neuron"),
            P("neuron"),
            P("tm"),
            P("neuron", None),
            P("neuron", None),
        ),
        out_specs=(P("tm", None), P("neuron")),
        check_vma=False,
    )
```

```python
import jax
import jax.numpy as jnp
from jax import lax
from jax.sharding import PartitionSpec as P

F32 = jnp.float32
BF16 = jnp.bfloat16
EXACT = lax.Precision.HIGHEST


def sum_rows(part, axis):
    count = lax.axis_size(axis)
    blocks = part.astype(BF16).reshape(count, part.shape[0] // count, part.shape[1])
    mine = lax.all_to_all(blocks, axis, 0, 0)
    return jnp.sum(mine.astype(F32), axis=0)


def spread(part, axis):
    count = lax.axis_size(axis)
    copies = jnp.broadcast_to(part[None], (count,) + part.shape)
    return lax.all_to_all(copies, axis, 0, 0)


def body(spikes, read_weight, in_proj, decay_rate, gate, out_fwd, out_bwd):
    bins = spikes.shape[1]
    blocks = lax.axis_size("tm")
    place = lax.axis_index("tm")
    log_gate = jnp.log(gate)
    row = lax.broadcasted_iota(jnp.int32, (bins, bins), 0)
    col = lax.broadcasted_iota(jnp.int32, (bins, bins), 1)
    upto = jnp.sum(jnp.where(col <= row, log_gate[None, :], 0.0), axis=1)
    before = upto - log_gate
    upto_t = jnp.sum(jnp.where(row <= col, log_gate[:, None], 0.0), axis=0)
    before_t = upto_t - log_gate
    mix_fwd = jnp.where(col <= row, jnp.exp(jnp.minimum(upto[:, None] - upto_t[None, :], 0.0)), 0.0)
    mix_bwd = jnp.where(col >= row, jnp.exp(jnp.minimum(before_t[None, :] - before[:, None], 0.0)), 0.0)
    time = (lax.broadcasted_iota(jnp.int32, (bins, 1), 0) - bins // 2).astype(F32)
    grow = jnp.exp(time * decay_rate[None, :])
    shrink = jnp.exp(-time * decay_rate[None, :])
    first = jnp.arange(bins, dtype=jnp.int32).astype(F32)[:, None]
    cum_fwd = jnp.exp(upto[:, None] - (first + 1.0) * decay_rate[None, :])
    cum_bwd = jnp.exp((upto[-1] - before)[:, None] - (bins - first) * decay_rate[None, :])
    scale_in = jnp.sqrt(-jnp.expm1(-2.0 * decay_rate))

    counts = spikes.astype(BF16)
    partial_sum = lax.dot_general(
        counts, read_weight, (((0,), (0,)), ((), ())), preferred_element_type=F32
    )
    rows = sum_rows(partial_sum, "neuron")
    power = jnp.mean(rows * rows, axis=-1, keepdims=True) + 1e-05
    normed_rows = (rows * lax.rsqrt(power)).astype(BF16)
    normed = spread(normed_rows, "neuron").reshape(bins, -1)

    drive = jnp.dot(normed, in_proj, preferred_element_type=F32) * scale_in[None, :]
    state_fwd = jnp.dot(mix_fwd, drive * grow, precision=EXACT) * shrink
    state_bwd = jnp.dot(mix_bwd, drive * shrink, precision=EXACT) * grow
    sent = jnp.stack([state_fwd[-1], state_bwd[0], jnp.broadcast_to(upto[-1], decay_rate.shape)])
    got = spread(sent, "tm")
    loss = got[:, 2, :]
    order = jnp.arange(blocks, dtype=jnp.int32)[:, None]
    earlier = (order >= order.T).astype(F32)
    span = jnp.sum(earlier[:, :, None] * loss[None, :, :], axis=1)
    span_before = span - loss
    at_fwd = jnp.sum(jnp.where(order == place, span_before, 0.0), axis=0)
    at_bwd = jnp.sum(jnp.where(order == place, span, 0.0), axis=0)
    gap_fwd = ((place - 1 - order) * bins).astype(F32) * decay_rate[None, :]
    gap_bwd = ((order - 1 - place) * bins).astype(F32) * decay_rate[None, :]
    weight_fwd = jnp.where(order < place, jnp.exp(jnp.minimum(at_fwd[None, :] - span - gap_fwd, 0.0)), 0.0)
    weight_bwd = jnp.where(order > place, jnp.exp(jnp.minimum(span_before - at_bwd[None, :] - gap_bwd, 0.0)), 0.0)
    enter_fwd = jnp.sum(weight_fwd * got[:, 0, :], axis=0)
    enter_bwd = jnp.sum(weight_bwd * got[:, 1, :], axis=0)
    forward = state_fwd + cum_fwd * enter_fwd[None, :]
    backward = state_bwd + cum_bwd * enter_bwd[None, :]
    mixed_part = jnp.dot(forward.astype(BF16), out_fwd, preferred_element_type=F32)
    mixed_part = mixed_part + jnp.dot(backward.astype(BF16), out_bwd, preferred_element_type=F32)
    mixed_rows = sum_rows(mixed_part, "neuron")
    latent_rows = (normed_rows.astype(F32) + mixed_rows).astype(BF16)
    latent = spread(latent_rows, "neuron").reshape(bins, -1)

    log_rate = lax.dot_general(
        read_weight, latent, (((1,), (1,)), ((), ())), preferred_element_type=F32
    )
    terms = jnp.exp(log_rate) - spikes.astype(F32) * log_rate
    part = jnp.sum(terms, axis=1).reshape(-1, 128)
    total = jnp.sum(spread(part.astype(BF16), "tm").astype(F32), axis=0).reshape(-1)
    nll = total / (bins * blocks)
    return (latent, nll)


def solution(mesh):
    return jax.shard_map(
        body,
        mesh=mesh,
        in_specs=(
            P("neuron", "tm"),
            P("neuron", None),
            P(None, "neuron"),
            P("neuron"),
            P("tm"),
            P("neuron", None),
            P("neuron", None),
        ),
        out_specs=(P("tm", None), P("neuron")),
        check_vma=False,
    )
```

```python
import jax
import jax.numpy as jnp
from jax import lax
from jax.experimental import pallas as pl
from jax.experimental.pallas import tpu as pltpu
from jax.sharding import PartitionSpec as P

F32 = jnp.float32
BF16 = jnp.bfloat16
ROWS = (((1,), (1,)), ((), ()))


def spread(part, axis):
    count = lax.axis_size(axis)
    copies = jnp.broadcast_to(part[None], (count,) + part.shape)
    return lax.all_to_all(copies, axis, 0, 0)


def powers(rate, bins, low, sign):
    fine = 16
    coarse = bins // fine
    a = lax.broadcasted_iota(jnp.int32, (coarse, 1), 0) * fine - low
    b = lax.broadcasted_iota(jnp.int32, (fine, 1), 0)
    big = jnp.exp(sign * (a.astype(F32) * rate))
    small = jnp.exp(sign * (b.astype(F32) * rate))
    return (big[:, None, :] * small[None, :, :]).reshape(bins, rate.shape[1])


def mix_kernel(normed, weights, enter, mix_fwd, mix_bwd, lead_fwd, lead_bwd, latent, total):
    turn = pl.program_id(0)
    bins = normed.shape[0]
    modes = weights.shape[1] // 3
    rows = normed[...]

    @pl.when(turn == 0)
    def _():
        total[...] = rows.astype(F32)

    acc = total[...]
    for pair in range(weights.shape[0] // 2):
        two = slice(2 * pair, 2 * pair + 2)

        def line(r):
            return jnp.concatenate([enter[2 * pair, r : r + 1, :], enter[2 * pair + 1, r : r + 1, :]], axis=1)

        rate = line(2)
        grow = powers(rate, bins, bins // 2, 1.0)
        shrink = powers(rate, bins, bins // 2, -1.0)
        proj = weights[two, :modes, :].reshape(2 * modes, -1)
        fwd_out = weights[two, modes : 2 * modes, :].reshape(2 * modes, -1)
        bwd_out = weights[two, 2 * modes :, :].reshape(2 * modes, -1)
        drive = lax.dot_general(rows, proj, ROWS, preferred_element_type=F32) * line(3)
        ahead = jnp.dot(mix_fwd[...], (drive * grow).astype(BF16), preferred_element_type=F32)
        behind = jnp.dot(mix_bwd[...], (drive * shrink).astype(BF16), preferred_element_type=F32)
        ahead = (ahead + lead_fwd[...] * line(0)) * shrink
        behind = (behind + lead_bwd[...] * line(1)) * grow
        acc = acc + jnp.dot(ahead.astype(BF16), fwd_out, preferred_element_type=F32)
        acc = acc + jnp.dot(behind.astype(BF16), bwd_out, preferred_element_type=F32)
    total[...] = acc

    @pl.when(turn == pl.num_programs(0) - 1)
    def _():
        latent[...] = acc.astype(BF16)


def mix_all(normed, weights, enter, mix_fwd, mix_bwd, lead_fwd, lead_bwd):
    bins, channels = normed.shape
    count = weights.shape[0]
    group = 4
    whole = lambda *shape: pl.BlockSpec(shape, lambda i: (0,) * len(shape))
    return pl.pallas_call(
        mix_kernel,
        grid=(count // group,),
        in_specs=[
            whole(bins, channels),
            pl.BlockSpec((group,) + weights.shape[1:], lambda i: (i, 0, 0)),
            pl.BlockSpec((group,) + enter.shape[1:], lambda i: (i, 0, 0)),
            whole(bins, bins),
            whole(bins, bins),
            whole(bins, 1),
            whole(bins, 1),
        ],
        out_specs=whole(bins, channels),
        out_shape=jax.ShapeDtypeStruct((bins, channels), BF16),
        scratch_shapes=[pltpu.VMEM((bins, channels), F32)],
        compiler_params=pltpu.CompilerParams(vmem_limit_bytes=32 * 1024 * 1024),
        name="mix_all",
    )(normed, weights, enter, mix_fwd, mix_bwd, lead_fwd, lead_bwd)


def body(spikes, read_weight, in_proj, decay_rate, gate, out_fwd, out_bwd):
    bins = spikes.shape[1]
    blocks = lax.axis_size("tm")
    place = lax.axis_index("tm")
    weights = lax.all_gather(jnp.concatenate([in_proj.T, out_fwd, out_bwd], axis=0), "neuron")
    log_gate = jnp.log(gate)
    row = lax.broadcasted_iota(jnp.int32, (bins, bins), 0)
    col = lax.broadcasted_iota(jnp.int32, (bins, bins), 1)
    upto = jnp.sum(jnp.where(col <= row, log_gate[None, :], 0.0), axis=1, keepdims=True)
    before = upto - log_gate[:, None]
    upto_t = jnp.sum(jnp.where(row <= col, log_gate[:, None], 0.0), axis=0, keepdims=True)
    before_t = upto_t - log_gate[None, :]
    mix_fwd = jnp.where(col <= row, jnp.exp(jnp.minimum(upto - upto_t, 0.0)), 0.0).astype(BF16)
    mix_bwd = jnp.where(col >= row, jnp.exp(jnp.minimum(before_t - before, 0.0)), 0.0).astype(BF16)
    whole = upto[bins - 1, 0]
    first = lax.broadcasted_iota(jnp.int32, (bins, 1), 0).astype(F32)
    rate = decay_rate[None, :]
    carry_fwd = jnp.exp((whole - upto) - (bins - 1 - first) * rate)
    carry_bwd = jnp.exp(before - first * rate)
    lead_fwd = jnp.exp(upto)
    lead_bwd = jnp.exp(whole - before)
    scale_in = jnp.sqrt(-jnp.expm1(-2.0 * decay_rate))

    counts = spikes.astype(BF16)
    partial_sum = lax.dot_general(
        counts, read_weight, (((0,), (0,)), ((), ())), preferred_element_type=F32
    )
    ring = lax.axis_size("neuron")
    parts = partial_sum.astype(BF16).reshape(ring, bins // ring, -1)
    rows = jnp.sum(lax.all_to_all(parts, "neuron", 0, 0).astype(F32), axis=0)
    power = jnp.mean(rows * rows, axis=-1, keepdims=True) + 1e-05
    normed_rows = (rows * lax.rsqrt(power)).astype(BF16)
    normed = spread(normed_rows, "neuron").reshape(bins, -1)

    drive = jnp.dot(normed, in_proj, preferred_element_type=F32)
    sent = jnp.stack(
        [
            jnp.sum(drive * carry_fwd, axis=0) * scale_in,
            jnp.sum(drive * carry_bwd, axis=0) * scale_in,
            jnp.broadcast_to(whole, decay_rate.shape),
        ]
    )
    got = spread(sent, "tm")
    loss = got[:, 2, :]
    order = jnp.arange(blocks, dtype=jnp.int32)[:, None]
    earlier = (order >= order.T).astype(F32)
    span = jnp.sum(earlier[:, :, None] * loss[None, :, :], axis=1)
    span_before = span - loss
    at_fwd = jnp.sum(jnp.where(order == place, span_before, 0.0), axis=0)
    at_bwd = jnp.sum(jnp.where(order == place, span, 0.0), axis=0)
    gap_fwd = ((place - 1 - order) * bins).astype(F32) * rate
    gap_bwd = ((order - 1 - place) * bins).astype(F32) * rate
    weight_fwd = jnp.where(order < place, jnp.exp(jnp.minimum(at_fwd[None, :] - span - gap_fwd, 0.0)), 0.0)
    weight_bwd = jnp.where(order > place, jnp.exp(jnp.minimum(span_before - at_bwd[None, :] - gap_bwd, 0.0)), 0.0)
    enter_fwd = jnp.sum(weight_fwd * got[:, 0, :], axis=0)
    enter_bwd = jnp.sum(weight_bwd * got[:, 1, :], axis=0)
    half = bins // 2
    enter = jnp.stack(
        [
            enter_fwd * jnp.exp(-(bins - half + 1.0) * decay_rate),
            enter_bwd * jnp.exp(-(bins - half) * decay_rate),
            decay_rate,
            scale_in,
        ]
    )
    latent = mix_all(normed, weights, spread(enter, "neuron"), mix_fwd, mix_bwd, lead_fwd, lead_bwd)

    log_rate = lax.dot_general(
        read_weight, latent, (((1,), (1,)), ((), ())), preferred_element_type=F32
    )
    terms = jnp.exp(log_rate) - spikes.astype(F32) * log_rate
    part = jnp.sum(terms, axis=1).reshape(-1, 128)
    total = jnp.sum(spread(part.astype(BF16), "tm").astype(F32), axis=0).reshape(-1)
    nll = total / (bins * blocks)
    return (latent, nll)


def solution(mesh):
    return jax.shard_map(
        body,
        mesh=mesh,
        in_specs=(
            P("neuron", "tm"),
            P("neuron", None),
            P(None, "neuron"),
            P("neuron"),
            P("tm"),
            P("neuron", None),
            P("neuron", None),
        ),
        out_specs=(P("tm", None), P("neuron")),
        check_vma=False,
    )
```

```python
import jax
import jax.numpy as jnp
from jax import lax
from jax.experimental import pallas as pl
from jax.experimental.pallas import tpu as pltpu
from jax.sharding import PartitionSpec as P

F32 = jnp.float32
BF16 = jnp.bfloat16
ROWS = (((1,), (1,)), ((), ()))
LANES = 128
ROOM = 40 * 1024 * 1024
IN_VMEM = pl.BlockSpec(memory_space=pltpu.VMEM)
IN_HBM = pl.BlockSpec(memory_space=pltpu.HBM)


def far(array):
    return pltpu.with_memory_space_constraint(array, pltpu.HBM)


def near(array):
    return pltpu.with_memory_space_constraint(array, pltpu.VMEM)


def spread(part, axis):
    count = lax.axis_size(axis)
    copies = jnp.broadcast_to(part[None], (count,) + part.shape)
    return lax.all_to_all(copies, axis, 0, 0)


def read_kernel(counts_far, weights_far, part, turned, counts, weights, arrived):
    chunks, _, tall = turned.shape
    copies = []
    for k in range(chunks):
        here = pl.ds(k * tall, tall)
        for far, near, which in ((counts_far, counts, 0), (weights_far, weights, 1)):
            copies.append(pltpu.make_async_copy(far.at[here], near.at[here], arrived.at[which, k]))
            copies[-1].start()
    acc = None
    for k in range(chunks):
        here = slice(k * tall, (k + 1) * tall)
        copies[2 * k].wait()
        columns = counts[here, :].astype(F32).astype(BF16).T
        turned[k] = columns
        copies[2 * k + 1].wait()
        one = jnp.dot(columns, weights[here, :], preferred_element_type=F32)
        acc = one if acc is None else acc + one
    part[...] = acc.astype(BF16).reshape(part.shape)


def read_in(spikes, read_weight, ring):
    neurons, bins = spikes.shape
    channels = read_weight.shape[1]
    chunks = 8
    return pl.pallas_call(
        read_kernel,
        in_specs=[IN_HBM, IN_HBM],
        out_specs=[IN_VMEM, IN_VMEM],
        out_shape=[
            jax.ShapeDtypeStruct((ring, bins // ring, channels), BF16),
            jax.ShapeDtypeStruct((chunks, bins, neurons // chunks), BF16),
        ],
        scratch_shapes=[
            pltpu.VMEM((neurons, bins), spikes.dtype),
            pltpu.VMEM((neurons, channels), BF16),
            pltpu.SemaphoreType.DMA((2, chunks)),
        ],
        compiler_params=pltpu.CompilerParams(vmem_limit_bytes=ROOM),
        name="read_in",
    )(far(spikes), far(read_weight))


def likelihood_kernel(latent, weights, turned_far, copies, out_latent, sums, turned, arrived):
    chunks, _, wide = turned.shape
    pieces = wide // LANES
    coming = [pltpu.make_async_copy(turned_far.at[k], turned.at[k], arrived.at[k]) for k in range(chunks)]
    for one in coming:
        one.start()
    rows = latent[...]
    out_latent[...] = rows
    for k in range(chunks):
        log_rate = lax.dot_general(
            rows, weights[k * wide : (k + 1) * wide, :], ROWS, preferred_element_type=F32
        )
        coming[k].wait()
        terms = jnp.exp(log_rate) - turned[k].astype(F32) * log_rate
        one = jnp.sum(terms, axis=0, keepdims=True)
        for j in range(pieces):
            sums[pieces * k + j : pieces * k + j + 1, :] = one[:, j * LANES : (j + 1) * LANES]
    small = sums[...].astype(BF16)
    copies[...] = jnp.broadcast_to(small[None], copies.shape)


def likelihood(latent, read_weight, turned, blocks):
    neurons = read_weight.shape[0]
    return pl.pallas_call(
        likelihood_kernel,
        in_specs=[IN_VMEM, IN_VMEM, IN_HBM],
        out_specs=[IN_VMEM, IN_VMEM],
        out_shape=[
            jax.ShapeDtypeStruct((blocks, neurons // LANES, LANES), BF16),
            jax.ShapeDtypeStruct(latent.shape, BF16),
        ],
        scratch_shapes=[
            pltpu.VMEM((neurons // LANES, LANES), F32),
            pltpu.VMEM(turned.shape, BF16),
            pltpu.SemaphoreType.DMA((turned.shape[0],)),
        ],
        compiler_params=pltpu.CompilerParams(vmem_limit_bytes=ROOM),
        name="likelihood",
    )(latent, read_weight, far(turned))


def body(spikes, read_weight, in_proj, decay_rate, gate, out_fwd, out_bwd):
    bins = spikes.shape[1]
    ring = lax.axis_size("neuron")
    blocks = lax.axis_size("tm")
    place = lax.axis_index("tm")
    log_gate = jnp.log(gate)
    row = lax.broadcasted_iota(jnp.int32, (bins, bins), 0)
    col = lax.broadcasted_iota(jnp.int32, (bins, bins), 1)
    upto = jnp.sum(jnp.where(col <= row, log_gate[None, :], 0.0), axis=1, keepdims=True)
    before = upto - log_gate[:, None]
    upto_t = jnp.sum(jnp.where(row <= col, log_gate[:, None], 0.0), axis=0, keepdims=True)
    before_t = upto_t - log_gate[None, :]
    mix_fwd = jnp.where(col <= row, jnp.exp(jnp.minimum(upto - upto_t, 0.0)), 0.0).astype(BF16)
    mix_bwd = jnp.where(col >= row, jnp.exp(jnp.minimum(before_t - before, 0.0)), 0.0).astype(BF16)
    whole = upto[bins - 1, 0]
    first = lax.broadcasted_iota(jnp.int32, (bins, 1), 0).astype(F32)
    rate = decay_rate[None, :]
    scale_in = jnp.sqrt(-jnp.expm1(-2.0 * rate))
    carry_fwd = jnp.exp((whole - upto) - (bins - 1 - first) * rate) * scale_in
    carry_bwd = jnp.exp(before - first * rate) * scale_in
    cum_fwd = jnp.exp(upto - (first + 1.0) * rate)
    cum_bwd = jnp.exp((whole - before) - (bins - first) * rate)
    grow = jnp.exp((first - bins // 2) * rate)
    shrink = jnp.exp((bins // 2 - first) * rate)

    parts, turned = read_in(spikes, read_weight, ring)
    rows = jnp.sum(lax.all_to_all(parts, "neuron", 0, 0).astype(F32), axis=0)
    power = jnp.mean(rows * rows, axis=-1, keepdims=True) + 1e-05
    normed_rows = (rows * lax.rsqrt(power)).astype(BF16)
    normed = spread(normed_rows, "neuron").reshape(bins, -1)

    drive = jnp.dot(normed, in_proj, preferred_element_type=F32)
    sent = jnp.stack(
        [
            jnp.sum(drive * carry_fwd, axis=0),
            jnp.sum(drive * carry_bwd, axis=0),
            jnp.broadcast_to(whole, decay_rate.shape),
        ]
    )
    got = spread(sent, "tm")
    drive = drive * scale_in
    state_fwd = jnp.dot(mix_fwd, (drive * grow).astype(BF16), preferred_element_type=F32) * shrink
    state_bwd = jnp.dot(mix_bwd, (drive * shrink).astype(BF16), preferred_element_type=F32) * grow

    loss = got[:, 2, :]
    order = jnp.arange(blocks, dtype=jnp.int32)[:, None]
    earlier = (order >= order.T).astype(F32)
    span = jnp.sum(earlier[:, :, None] * loss[None, :, :], axis=1)
    span_before = span - loss
    at_fwd = jnp.sum(jnp.where(order == place, span_before, 0.0), axis=0)
    at_bwd = jnp.sum(jnp.where(order == place, span, 0.0), axis=0)
    gap_fwd = ((place - 1 - order) * bins).astype(F32) * rate
    gap_bwd = ((order - 1 - place) * bins).astype(F32) * rate
    weight_fwd = jnp.where(order < place, jnp.exp(jnp.minimum(at_fwd[None, :] - span - gap_fwd, 0.0)), 0.0)
    weight_bwd = jnp.where(order > place, jnp.exp(jnp.minimum(span_before - at_bwd[None, :] - gap_bwd, 0.0)), 0.0)
    enter_fwd = jnp.sum(weight_fwd * got[:, 0, :], axis=0)
    enter_bwd = jnp.sum(weight_bwd * got[:, 1, :], axis=0)
    forward = (state_fwd + cum_fwd * enter_fwd[None, :]).astype(BF16)
    backward = (state_bwd + cum_bwd * enter_bwd[None, :]).astype(BF16)
    mixed = jnp.dot(forward, out_fwd, preferred_element_type=F32)
    mixed = mixed + jnp.dot(backward, out_bwd, preferred_element_type=F32)
    parts = mixed.astype(BF16).reshape(ring, bins // ring, -1)
    mixed_rows = jnp.sum(lax.all_to_all(parts, "neuron", 0, 0).astype(F32), axis=0)
    latent_rows = (normed_rows.astype(F32) + mixed_rows).astype(BF16)
    latent = spread(latent_rows, "neuron").reshape(bins, -1)

    copies, latent = likelihood(latent, read_weight, turned, blocks)
    terms = lax.all_to_all(copies, "tm", 0, 0)
    nll = jnp.sum(terms.astype(F32), axis=0).reshape(-1) * (1.0 / (bins * blocks))
    return (latent, nll)


def solution(mesh):
    return jax.shard_map(
        body,
        mesh=mesh,
        in_specs=(
            P("neuron", "tm"),
            P("neuron", None),
            P(None, "neuron"),
            P("neuron"),
            P("tm"),
            P("neuron", None),
            P("neuron", None),
        ),
        out_specs=(P("tm", None), P("neuron")),
        check_vma=False,
    )
```

```python
import jax
import jax.numpy as jnp
from jax import lax
from jax.experimental import pallas as pl
from jax.experimental.pallas import tpu as pltpu
from jax.sharding import PartitionSpec as P

F32 = jnp.float32
BF16 = jnp.bfloat16
ROWS = (((1,), (1,)), ((), ()))
COLUMNS = (((0,), (0,)), ((), ()))
LANES = 128
ROOM = 14 * 1024 * 1024
IN_VMEM = pl.BlockSpec(memory_space=pltpu.VMEM)
IN_HBM = pl.BlockSpec(memory_space=pltpu.HBM)


def far(array):
    return pltpu.with_memory_space_constraint(array, pltpu.HBM)


def near(array):
    return pltpu.with_memory_space_constraint(array, pltpu.VMEM)


def spread(part, axis):
    count = lax.axis_size(axis)
    copies = jnp.broadcast_to(part[None], (count,) + part.shape)
    return lax.all_to_all(copies, axis, 0, 0)


def read_kernel(counts_far, weights_far, part, counts, weights, arrived):
    chunks = arrived.shape[1]
    tall = counts.shape[0] // chunks
    copies = []
    for k in range(chunks):
        here = pl.ds(k * tall, tall)
        for away, here_ref, which in ((counts_far, counts, 0), (weights_far, weights, 1)):
            copies.append(pltpu.make_async_copy(away.at[here], here_ref.at[here], arrived.at[which, k]))
            copies[-1].start()
    acc = None
    for k in range(chunks):
        here = slice(k * tall, (k + 1) * tall)
        copies[2 * k].wait()
        copies[2 * k + 1].wait()
        rows = counts[here, :].astype(F32).astype(BF16)
        one = lax.dot_general(rows, weights[here, :], COLUMNS, preferred_element_type=F32)
        acc = one if acc is None else acc + one
    part[...] = acc.astype(BF16).reshape(part.shape)


def read_in(spikes, read_weight, ring):
    neurons, bins = spikes.shape
    channels = read_weight.shape[1]
    return pl.pallas_call(
        read_kernel,
        in_specs=[IN_HBM, IN_HBM],
        out_specs=IN_VMEM,
        out_shape=jax.ShapeDtypeStruct((ring, bins // ring, channels), BF16),
        scratch_shapes=[
            pltpu.VMEM((neurons, bins), spikes.dtype),
            pltpu.VMEM((neurons, channels), BF16),
            pltpu.SemaphoreType.DMA((2, 8)),
        ],
        compiler_params=pltpu.CompilerParams(vmem_limit_bytes=ROOM),
        name="read_in",
    )(far(spikes), far(read_weight))


def turn_kernel(counts_far, after, turned, counts, arrived):
    chunks, _, tall = turned.shape
    coming = []
    for k in range(chunks):
        here = pl.ds(k * tall, tall)
        coming.append(pltpu.make_async_copy(counts_far.at[here], counts.at[here], arrived.at[k]))
        coming[-1].start()
    for k in range(chunks):
        coming[k].wait()
        turned[k] = counts[k * tall : (k + 1) * tall, :].astype(F32).astype(BF16).T


def turn(spikes, after):
    neurons, bins = spikes.shape
    chunks = 8
    turned = (chunks, bins, neurons // chunks)
    return pl.pallas_call(
        turn_kernel,
        in_specs=[IN_HBM, pl.BlockSpec(memory_space=pl.ANY)],
        out_specs=IN_VMEM,
        out_shape=pltpu.VMEM(turned, BF16),
        scratch_shapes=[
            pltpu.VMEM((neurons, bins), spikes.dtype),
            pltpu.SemaphoreType.DMA((chunks,)),
        ],
        compiler_params=pltpu.CompilerParams(vmem_limit_bytes=ROOM),
        name="turn",
    )(far(spikes), after)


def likelihood_kernel(latent, weights, turned, copies, out_latent, sums):
    chunks, _, wide = turned.shape
    pieces = wide // LANES
    rows = latent[...]
    out_latent[...] = rows
    for k in range(chunks):
        log_rate = lax.dot_general(
            rows, weights[k * wide : (k + 1) * wide, :], ROWS, preferred_element_type=F32
        )
        terms = jnp.exp(log_rate) - turned[k].astype(F32) * log_rate
        one = jnp.sum(terms, axis=0, keepdims=True)
        for j in range(pieces):
            sums[pieces * k + j : pieces * k + j + 1, :] = one[:, j * LANES : (j + 1) * LANES]
    small = sums[...].astype(BF16)
    copies[...] = jnp.broadcast_to(small[None], copies.shape)


def likelihood(latent, read_weight, turned, blocks):
    neurons = read_weight.shape[0]
    return pl.pallas_call(
        likelihood_kernel,
        in_specs=[IN_VMEM, IN_VMEM, IN_VMEM],
        out_specs=[IN_VMEM, IN_VMEM],
        out_shape=[
            jax.ShapeDtypeStruct((blocks, neurons // LANES, LANES), BF16),
            jax.ShapeDtypeStruct(latent.shape, BF16),
        ],
        scratch_shapes=[
            pltpu.VMEM((neurons // LANES, LANES), F32),
        ],
        compiler_params=pltpu.CompilerParams(vmem_limit_bytes=ROOM),
        name="likelihood",
    )(near(latent), near(read_weight), near(turned))


def body(spikes, read_weight, in_proj, decay_rate, gate, out_fwd, out_bwd):
    bins = spikes.shape[1]
    ring = lax.axis_size("neuron")
    blocks = lax.axis_size("tm")
    place = lax.axis_index("tm")
    log_gate = jnp.log(gate)
    row = lax.broadcasted_iota(jnp.int32, (bins, bins), 0)
    col = lax.broadcasted_iota(jnp.int32, (bins, bins), 1)
    upto = jnp.sum(jnp.where(col <= row, log_gate[None, :], 0.0), axis=1, keepdims=True)
    before = upto - log_gate[:, None]
    upto_t = jnp.sum(jnp.where(row <= col, log_gate[:, None], 0.0), axis=0, keepdims=True)
    before_t = upto_t - log_gate[None, :]
    mix_fwd = jnp.where(col <= row, jnp.exp(jnp.minimum(upto - upto_t, 0.0)), 0.0).astype(BF16)
    mix_bwd = jnp.where(col >= row, jnp.exp(jnp.minimum(before_t - before, 0.0)), 0.0).astype(BF16)
    whole = upto[bins - 1, 0]
    first = lax.broadcasted_iota(jnp.int32, (bins, 1), 0).astype(F32)
    rate = decay_rate[None, :]
    scale_in = jnp.sqrt(-jnp.expm1(-2.0 * rate))
    carry_fwd = jnp.exp((whole - upto) - (bins - 1 - first) * rate) * scale_in
    carry_bwd = jnp.exp(before - first * rate) * scale_in
    cum_fwd = jnp.exp(upto - (first + 1.0) * rate)
    cum_bwd = jnp.exp((whole - before) - (bins - first) * rate)
    grow = jnp.exp((first - bins // 2) * rate)
    shrink = jnp.exp((bins // 2 - first) * rate)

    parts = read_in(spikes, read_weight, ring)
    rows = jnp.sum(lax.all_to_all(parts, "neuron", 0, 0).astype(F32), axis=0)
    power = jnp.mean(rows * rows, axis=-1, keepdims=True) + 1e-05
    normed_rows = (rows * lax.rsqrt(power)).astype(BF16)
    normed = spread(normed_rows, "neuron").reshape(bins, -1)
    turned = turn(spikes, normed_rows)

    drive = jnp.dot(normed, in_proj, preferred_element_type=F32)
    sent = jnp.stack(
        [
            jnp.sum(drive * carry_fwd, axis=0),
            jnp.sum(drive * carry_bwd, axis=0),
            jnp.broadcast_to(whole, decay_rate.shape),
        ]
    )
    got = spread(sent, "tm")
    drive = drive * scale_in
    state_fwd = jnp.dot(mix_fwd, (drive * grow).astype(BF16), preferred_element_type=F32) * shrink
    state_bwd = jnp.dot(mix_bwd, (drive * shrink).astype(BF16), preferred_element_type=F32) * grow

    loss = got[:, 2, :]
    order = jnp.arange(blocks, dtype=jnp.int32)[:, None]
    earlier = (order >= order.T).astype(F32)
    span = jnp.sum(earlier[:, :, None] * loss[None, :, :], axis=1)
    span_before = span - loss
    at_fwd = jnp.sum(jnp.where(order == place, span_before, 0.0), axis=0)
    at_bwd = jnp.sum(jnp.where(order == place, span, 0.0), axis=0)
    gap_fwd = ((place - 1 - order) * bins).astype(F32) * rate
    gap_bwd = ((order - 1 - place) * bins).astype(F32) * rate
    weight_fwd = jnp.where(order < place, jnp.exp(jnp.minimum(at_fwd[None, :] - span - gap_fwd, 0.0)), 0.0)
    weight_bwd = jnp.where(order > place, jnp.exp(jnp.minimum(span_before - at_bwd[None, :] - gap_bwd, 0.0)), 0.0)
    enter_fwd = jnp.sum(weight_fwd * got[:, 0, :], axis=0)
    enter_bwd = jnp.sum(weight_bwd * got[:, 1, :], axis=0)
    forward = (state_fwd + cum_fwd * enter_fwd[None, :]).astype(BF16)
    backward = (state_bwd + cum_bwd * enter_bwd[None, :]).astype(BF16)
    mixed = jnp.dot(forward, out_fwd, preferred_element_type=F32)
    mixed = mixed + jnp.dot(backward, out_bwd, preferred_element_type=F32)
    parts = mixed.astype(BF16).reshape(ring, bins // ring, -1)
    mixed_rows = jnp.sum(lax.all_to_all(parts, "neuron", 0, 0).astype(F32), axis=0)
    latent_rows = (normed_rows.astype(F32) + mixed_rows).astype(BF16)
    latent = spread(latent_rows, "neuron").reshape(bins, -1)

    copies, latent = likelihood(latent, read_weight, turned, blocks)
    terms = lax.all_to_all(copies, "tm", 0, 0)
    nll = jnp.sum(terms.astype(F32), axis=0).reshape(-1) * (1.0 / (bins * blocks))
    return (latent, nll)


def solution(mesh):
    return jax.shard_map(
        body,
        mesh=mesh,
        in_specs=(
            P("neuron", "tm"),
            P("neuron", None),
            P(None, "neuron"),
            P("neuron"),
            P("tm"),
            P("neuron", None),
            P("neuron", None),
        ),
        out_specs=(P("tm", None), P("neuron")),
        check_vma=False,
    )
```

```python
import jax
import jax.numpy as jnp
from jax import lax
from jax.experimental import pallas as pl
from jax.experimental.pallas import tpu as pltpu
from jax.sharding import Mesh
from jax.sharding import PartitionSpec as P

F32 = jnp.float32
BF16 = jnp.bfloat16
ROWS = (((1,), (1,)), ((), ()))
COLUMNS = (((0,), (0,)), ((), ()))
LANES = 128
ROOM = 14 * 1024 * 1024
IN_VMEM = pl.BlockSpec(memory_space=pltpu.VMEM)
IN_HBM = pl.BlockSpec(memory_space=pltpu.HBM)


def far(array):
    return pltpu.with_memory_space_constraint(array, pltpu.HBM)


def near(array):
    return pltpu.with_memory_space_constraint(array, pltpu.VMEM)


def spread(part, axis):
    count = lax.axis_size(axis)
    copies = jnp.broadcast_to(part[None], (count,) + part.shape)
    return lax.all_to_all(copies, axis, 0, 0)


def reduce_rows(parts):
    quarter = jnp.sum(lax.all_to_all(parts, "near", 0, 0).astype(F32), axis=0)
    return jnp.sum(spread(quarter.astype(BF16), "far").astype(F32), axis=0)


def read_kernel(counts_far, weights_far, part, counts, weights, arrived):
    chunks = arrived.shape[1]
    tall = counts.shape[0] // chunks
    copies = []
    for k in range(chunks):
        here = pl.ds(k * tall, tall)
        for away, here_ref, which in ((counts_far, counts, 0), (weights_far, weights, 1)):
            copies.append(pltpu.make_async_copy(away.at[here], here_ref.at[here], arrived.at[which, k]))
            copies[-1].start()
    acc = None
    for k in range(chunks):
        here = slice(k * tall, (k + 1) * tall)
        copies[2 * k].wait()
        copies[2 * k + 1].wait()
        rows = counts[here, :].astype(F32).astype(BF16)
        one = lax.dot_general(rows, weights[here, :], COLUMNS, preferred_element_type=F32)
        acc = one if acc is None else acc + one
    part[...] = acc.astype(BF16).reshape(part.shape)


def read_in(spikes, read_weight, ring):
    neurons, bins = spikes.shape
    channels = read_weight.shape[1]
    return pl.pallas_call(
        read_kernel,
        in_specs=[IN_HBM, IN_HBM],
        out_specs=IN_VMEM,
        out_shape=jax.ShapeDtypeStruct((ring, bins // ring, channels), BF16),
        scratch_shapes=[
            pltpu.VMEM((neurons, bins), spikes.dtype),
            pltpu.VMEM((neurons, channels), BF16),
            pltpu.SemaphoreType.DMA((2, 8)),
        ],
        compiler_params=pltpu.CompilerParams(vmem_limit_bytes=ROOM),
        name="read_in",
    )(far(spikes), far(read_weight))


def turn_kernel(counts_far, after, turned_far, counts, turned, arrived, left):
    chunks, _, tall = turned.shape
    coming, leaving = [], []
    for k in range(chunks):
        here = pl.ds(k * tall, tall)
        coming.append(pltpu.make_async_copy(counts_far.at[here], counts.at[here], arrived.at[k]))
        leaving.append(pltpu.make_async_copy(turned.at[k], turned_far.at[k], left.at[k]))
        coming[-1].start()
    for k in range(chunks):
        coming[k].wait()
        turned[k] = counts[k * tall : (k + 1) * tall, :].astype(F32).astype(BF16).T
        leaving[k].start()
    for one in leaving:
        one.wait()


def turn(spikes, after):
    neurons, bins = spikes.shape
    chunks = 8
    turned = (chunks, bins, neurons // chunks)
    return pl.pallas_call(
        turn_kernel,
        in_specs=[IN_HBM, pl.BlockSpec(memory_space=pl.ANY)],
        out_specs=IN_HBM,
        out_shape=pltpu.HBM(turned, BF16),
        scratch_shapes=[
            pltpu.VMEM((neurons, bins), spikes.dtype),
            pltpu.VMEM(turned, BF16),
            pltpu.SemaphoreType.DMA((chunks,)),
            pltpu.SemaphoreType.DMA((chunks,)),
        ],
        compiler_params=pltpu.CompilerParams(vmem_limit_bytes=ROOM),
        name="turn",
    )(far(spikes), after)


def likelihood_kernel(latent, weights, turned_far, copies, out_latent, sums, turned, arrived):
    chunks, _, wide = turned.shape
    pieces = wide // LANES
    coming = [pltpu.make_async_copy(turned_far.at[k], turned.at[k], arrived.at[k]) for k in range(chunks)]
    for one in coming:
        one.start()
    rows = latent[...]
    out_latent[...] = rows
    for k in range(chunks):
        log_rate = lax.dot_general(
            rows, weights[k * wide : (k + 1) * wide, :], ROWS, preferred_element_type=F32
        )
        coming[k].wait()
        terms = jnp.exp(log_rate) - turned[k].astype(F32) * log_rate
        one = jnp.sum(terms, axis=0, keepdims=True)
        for j in range(pieces):
            sums[pieces * k + j : pieces * k + j + 1, :] = one[:, j * LANES : (j + 1) * LANES]
    small = sums[...].astype(BF16)
    copies[...] = jnp.broadcast_to(small[None], copies.shape)


def likelihood(latent, read_weight, turned, blocks):
    neurons = read_weight.shape[0]
    return pl.pallas_call(
        likelihood_kernel,
        in_specs=[IN_VMEM, IN_VMEM, IN_HBM],
        out_specs=[IN_VMEM, IN_VMEM],
        out_shape=[
            jax.ShapeDtypeStruct((blocks, neurons // LANES, LANES), BF16),
            jax.ShapeDtypeStruct(latent.shape, BF16),
        ],
        scratch_shapes=[
            pltpu.VMEM((neurons // LANES, LANES), F32),
            pltpu.VMEM(turned.shape, BF16),
            pltpu.SemaphoreType.DMA((turned.shape[0],)),
        ],
        compiler_params=pltpu.CompilerParams(vmem_limit_bytes=ROOM),
        name="likelihood",
    )(near(latent), near(read_weight), far(turned))


def body(spikes, read_weight, in_proj, decay_rate, gate, out_fwd, out_bwd):
    bins = spikes.shape[1]
    quad = lax.axis_size("near")
    blocks = lax.axis_size("tm")
    place = lax.axis_index("tm")
    log_gate = jnp.log(gate)
    row = lax.broadcasted_iota(jnp.int32, (bins, bins), 0)
    col = lax.broadcasted_iota(jnp.int32, (bins, bins), 1)
    upto = jnp.sum(jnp.where(col <= row, log_gate[None, :], 0.0), axis=1, keepdims=True)
    before = upto - log_gate[:, None]
    upto_t = jnp.sum(jnp.where(row <= col, log_gate[:, None], 0.0), axis=0, keepdims=True)
    before_t = upto_t - log_gate[None, :]
    mix_fwd = jnp.where(col <= row, jnp.exp(jnp.minimum(upto - upto_t, 0.0)), 0.0).astype(BF16)
    mix_bwd = jnp.where(col >= row, jnp.exp(jnp.minimum(before_t - before, 0.0)), 0.0).astype(BF16)
    whole = upto[bins - 1, 0]
    first = lax.broadcasted_iota(jnp.int32, (bins, 1), 0).astype(F32)
    rate = decay_rate[None, :]
    scale_in = jnp.sqrt(-jnp.expm1(-2.0 * rate))
    carry_fwd = jnp.exp((whole - upto) - (bins - 1 - first) * rate) * scale_in
    carry_bwd = jnp.exp(before - first * rate) * scale_in
    cum_fwd = jnp.exp(upto - (first + 1.0) * rate)
    cum_bwd = jnp.exp((whole - before) - (bins - first) * rate)
    grow = jnp.exp((first - bins // 2) * rate)
    shrink = jnp.exp((bins // 2 - first) * rate)

    rows = reduce_rows(read_in(spikes, read_weight, quad))
    power = jnp.mean(rows * rows, axis=-1, keepdims=True) + 1e-05
    normed_rows = (rows * lax.rsqrt(power)).astype(BF16)
    normed = spread(normed_rows, "near").reshape(bins, -1)
    turned = turn(spikes, normed_rows)

    drive = jnp.dot(normed, in_proj, preferred_element_type=F32)
    sent = jnp.stack(
        [
            jnp.sum(drive * carry_fwd, axis=0),
            jnp.sum(drive * carry_bwd, axis=0),
            jnp.broadcast_to(whole, decay_rate.shape),
        ]
    )
    got = spread(sent, "tm")
    drive = drive * scale_in
    state_fwd = jnp.dot(mix_fwd, (drive * grow).astype(BF16), preferred_element_type=F32) * shrink
    state_bwd = jnp.dot(mix_bwd, (drive * shrink).astype(BF16), preferred_element_type=F32) * grow

    loss = got[:, 2, :]
    order = jnp.arange(blocks, dtype=jnp.int32)[:, None]
    earlier = (order >= order.T).astype(F32)
    span = jnp.sum(earlier[:, :, None] * loss[None, :, :], axis=1)
    span_before = span - loss
    at_fwd = jnp.sum(jnp.where(order == place, span_before, 0.0), axis=0)
    at_bwd = jnp.sum(jnp.where(order == place, span, 0.0), axis=0)
    gap_fwd = ((place - 1 - order) * bins).astype(F32) * rate
    gap_bwd = ((order - 1 - place) * bins).astype(F32) * rate
    weight_fwd = jnp.where(order < place, jnp.exp(jnp.minimum(at_fwd[None, :] - span - gap_fwd, 0.0)), 0.0)
    weight_bwd = jnp.where(order > place, jnp.exp(jnp.minimum(span_before - at_bwd[None, :] - gap_bwd, 0.0)), 0.0)
    enter_fwd = jnp.sum(weight_fwd * got[:, 0, :], axis=0)
    enter_bwd = jnp.sum(weight_bwd * got[:, 1, :], axis=0)
    forward = (state_fwd + cum_fwd * enter_fwd[None, :]).astype(BF16)
    backward = (state_bwd + cum_bwd * enter_bwd[None, :]).astype(BF16)
    mixed = jnp.dot(forward, out_fwd, preferred_element_type=F32)
    mixed = mixed + jnp.dot(backward, out_bwd, preferred_element_type=F32)
    mixed_rows = reduce_rows(mixed.astype(BF16).reshape(quad, bins // quad, -1))
    latent_rows = (normed_rows.astype(F32) + mixed_rows).astype(BF16)
    latent = spread(latent_rows, "near").reshape(bins, -1)

    copies, latent = likelihood(latent, read_weight, turned, blocks)
    terms = lax.all_to_all(copies, "tm", 0, 0)
    nll = jnp.sum(terms.astype(F32), axis=0).reshape(-1) * (1.0 / (bins * blocks))
    return (latent, nll)


def solution(mesh):
    ring = mesh.shape["neuron"]
    quads = Mesh(mesh.devices.reshape(ring // 4, 4, -1), ("far", "near", "tm"))
    neuron = ("far", "near")
    return jax.shard_map(
        body,
        mesh=quads,
        in_specs=(
            P(neuron, "tm"),
            P(neuron, None),
            P(None, neuron),
            P(neuron),
            P("tm"),
            P(neuron, None),
            P(neuron, None),
        ),
        out_specs=(P("tm", None), P(neuron)),
        check_vma=False,
    )
```

```python
import jax
import jax.numpy as jnp
from jax import lax
from jax.experimental import pallas as pl
from jax.experimental.pallas import tpu as pltpu
from jax.sharding import Mesh
from jax.sharding import PartitionSpec as P

F32 = jnp.float32
BF16 = jnp.bfloat16
ROWS = (((1,), (1,)), ((), ()))
COLUMNS = (((0,), (0,)), ((), ()))
LANES = 128
ROOM = 14 * 1024 * 1024
IN_VMEM = pl.BlockSpec(memory_space=pltpu.VMEM)
IN_HBM = pl.BlockSpec(memory_space=pltpu.HBM)
ANYWHERE = pl.BlockSpec(memory_space=pl.ANY)


def far(array):
    return pltpu.with_memory_space_constraint(array, pltpu.HBM)


def near(array):
    return pltpu.with_memory_space_constraint(array, pltpu.VMEM)


def spread(part, axis):
    count = lax.axis_size(axis)
    copies = jnp.broadcast_to(part[None], (count,) + part.shape)
    return lax.all_to_all(copies, axis, 0, 0)


def reduce_rows(parts):
    quarter = jnp.sum(lax.all_to_all(parts, "near", 0, 0).astype(F32), axis=0)
    return jnp.sum(spread(quarter.astype(BF16), "far").astype(F32), axis=0)


def read_kernel(counts_far, weights_far, part, counts, weights, arrived):
    chunks = arrived.shape[1]
    tall = counts.shape[0] // chunks
    copies = []
    for k in range(chunks):
        here = pl.ds(k * tall, tall)
        for away, here_ref, which in ((counts_far, counts, 0), (weights_far, weights, 1)):
            copies.append(pltpu.make_async_copy(away.at[here], here_ref.at[here], arrived.at[which, k]))
            copies[-1].start()
    acc = None
    for k in range(chunks):
        here = slice(k * tall, (k + 1) * tall)
        copies[2 * k].wait()
        copies[2 * k + 1].wait()
        rows = counts[here, :].astype(F32).astype(BF16)
        one = lax.dot_general(rows, weights[here, :], COLUMNS, preferred_element_type=F32)
        acc = one if acc is None else acc + one
    part[...] = acc.astype(BF16).reshape(part.shape)


def read_in(spikes, read_weight, ring):
    neurons, bins = spikes.shape
    channels = read_weight.shape[1]
    return pl.pallas_call(
        read_kernel,
        in_specs=[IN_HBM, IN_HBM],
        out_specs=IN_VMEM,
        out_shape=jax.ShapeDtypeStruct((ring, bins // ring, channels), BF16),
        scratch_shapes=[
            pltpu.VMEM((neurons, bins), spikes.dtype),
            pltpu.VMEM((neurons, channels), BF16),
            pltpu.SemaphoreType.DMA((2, 8)),
        ],
        compiler_params=pltpu.CompilerParams(vmem_limit_bytes=ROOM),
        name="read_in",
    )(far(spikes), far(read_weight))


def narrow_kernel(counts_far, after, narrow, counts, arrived):
    chunks = arrived.shape[0]
    tall = counts.shape[0] // chunks
    coming = []
    for k in range(chunks):
        here = pl.ds(k * tall, tall)
        coming.append(pltpu.make_async_copy(counts_far.at[here], counts.at[here], arrived.at[k]))
        coming[-1].start()
    for k in range(chunks):
        coming[k].wait()
        here = slice(k * tall, (k + 1) * tall)
        narrow[here, :] = counts[here, :].astype(jnp.int8)


def narrowed(spikes, after):
    return pl.pallas_call(
        narrow_kernel,
        in_specs=[IN_HBM, ANYWHERE],
        out_specs=IN_VMEM,
        out_shape=pltpu.VMEM(spikes.shape, jnp.int8),
        scratch_shapes=[
            pltpu.VMEM(spikes.shape, spikes.dtype),
            pltpu.SemaphoreType.DMA((8,)),
        ],
        compiler_params=pltpu.CompilerParams(vmem_limit_bytes=ROOM),
        name="narrow",
    )(far(spikes), after)


def likelihood_kernel(latent, weights, counts, copies, out_latent, sums):
    wide = 4 * LANES
    rows = latent[...]
    out_latent[...] = rows
    for k in range(weights.shape[0] // wide):
        here = slice(k * wide, (k + 1) * wide)
        log_rate = lax.dot_general(weights[here, :], rows, ROWS, preferred_element_type=F32)
        terms = jnp.exp(log_rate) - counts[here, :].astype(F32) * log_rate
        folded = sum(terms[:, j : j + LANES] for j in range(0, rows.shape[0], LANES))
        for j in range(4):
            turned = folded[j * LANES : (j + 1) * LANES, :].T
            sums[4 * k + j : 4 * k + j + 1, :] = jnp.sum(turned, axis=0, keepdims=True)
    small = sums[...].astype(BF16)
    copies[...] = jnp.broadcast_to(small[None], copies.shape)


def likelihood(latent, read_weight, spikes, blocks):
    neurons = read_weight.shape[0]
    return pl.pallas_call(
        likelihood_kernel,
        in_specs=[IN_VMEM, IN_VMEM, IN_VMEM],
        out_specs=[IN_VMEM, IN_VMEM],
        out_shape=[
            jax.ShapeDtypeStruct((blocks, neurons // LANES, LANES), BF16),
            jax.ShapeDtypeStruct(latent.shape, BF16),
        ],
        scratch_shapes=[pltpu.VMEM((neurons // LANES, LANES), F32)],
        compiler_params=pltpu.CompilerParams(vmem_limit_bytes=ROOM),
        name="likelihood",
    )(near(latent), near(read_weight), near(spikes))


def body(spikes, read_weight, in_proj, decay_rate, gate, out_fwd, out_bwd):
    bins = spikes.shape[1]
    quad = lax.axis_size("near")
    blocks = lax.axis_size("tm")
    place = lax.axis_index("tm")
    log_gate = jnp.log(gate)
    row = lax.broadcasted_iota(jnp.int32, (bins, bins), 0)
    col = lax.broadcasted_iota(jnp.int32, (bins, bins), 1)
    upto = jnp.sum(jnp.where(col <= row, log_gate[None, :], 0.0), axis=1, keepdims=True)
    before = upto - log_gate[:, None]
    upto_t = jnp.sum(jnp.where(row <= col, log_gate[:, None], 0.0), axis=0, keepdims=True)
    before_t = upto_t - log_gate[None, :]
    mix_fwd = jnp.where(col <= row, jnp.exp(jnp.minimum(upto - upto_t, 0.0)), 0.0).astype(BF16)
    mix_bwd = jnp.where(col >= row, jnp.exp(jnp.minimum(before_t - before, 0.0)), 0.0).astype(BF16)
    whole = upto[bins - 1, 0]
    first = lax.broadcasted_iota(jnp.int32, (bins, 1), 0).astype(F32)
    rate = decay_rate[None, :]
    scale_in = jnp.sqrt(-jnp.expm1(-2.0 * rate))
    carry_fwd = jnp.exp((whole - upto) - (bins - 1 - first) * rate) * scale_in
    carry_bwd = jnp.exp(before - first * rate) * scale_in
    cum_fwd = jnp.exp(upto - (first + 1.0) * rate)
    cum_bwd = jnp.exp((whole - before) - (bins - first) * rate)
    grow = jnp.exp((first - bins // 2) * rate)
    shrink = jnp.exp((bins // 2 - first) * rate)

    rows = reduce_rows(read_in(spikes, read_weight, quad))
    power = jnp.mean(rows * rows, axis=-1, keepdims=True) + 1e-05
    normed_rows = (rows * lax.rsqrt(power)).astype(BF16)
    normed = spread(normed_rows, "near").reshape(bins, -1)

    drive = jnp.dot(normed, in_proj, preferred_element_type=F32)
    sent = jnp.stack(
        [
            jnp.sum(drive * carry_fwd, axis=0),
            jnp.sum(drive * carry_bwd, axis=0),
            jnp.broadcast_to(whole, decay_rate.shape),
        ]
    )
    got = spread(sent, "tm")
    drive = drive * scale_in
    state_fwd = jnp.dot(mix_fwd, (drive * grow).astype(BF16), preferred_element_type=F32) * shrink
    state_bwd = jnp.dot(mix_bwd, (drive * shrink).astype(BF16), preferred_element_type=F32) * grow

    loss = got[:, 2, :]
    order = jnp.arange(blocks, dtype=jnp.int32)[:, None]
    earlier = (order >= order.T).astype(F32)
    span = jnp.sum(earlier[:, :, None] * loss[None, :, :], axis=1)
    span_before = span - loss
    at_fwd = jnp.sum(jnp.where(order == place, span_before, 0.0), axis=0)
    at_bwd = jnp.sum(jnp.where(order == place, span, 0.0), axis=0)
    gap_fwd = ((place - 1 - order) * bins).astype(F32) * rate
    gap_bwd = ((order - 1 - place) * bins).astype(F32) * rate
    weight_fwd = jnp.where(order < place, jnp.exp(jnp.minimum(at_fwd[None, :] - span - gap_fwd, 0.0)), 0.0)
    weight_bwd = jnp.where(order > place, jnp.exp(jnp.minimum(span_before - at_bwd[None, :] - gap_bwd, 0.0)), 0.0)
    enter_fwd = jnp.sum(weight_fwd * got[:, 0, :], axis=0)
    enter_bwd = jnp.sum(weight_bwd * got[:, 1, :], axis=0)
    forward = (state_fwd + cum_fwd * enter_fwd[None, :]).astype(BF16)
    backward = (state_bwd + cum_bwd * enter_bwd[None, :]).astype(BF16)
    mixed = jnp.dot(forward, out_fwd, preferred_element_type=F32)
    mixed = mixed + jnp.dot(backward, out_bwd, preferred_element_type=F32)
    counts = narrowed(spikes, sent)
    mixed, counts = lax.optimization_barrier((mixed, counts))
    mixed_rows = reduce_rows(mixed.astype(BF16).reshape(quad, bins // quad, -1))
    latent_rows = (normed_rows.astype(F32) + mixed_rows).astype(BF16)
    latent = spread(latent_rows, "near").reshape(bins, -1)

    copies, latent = likelihood(latent, read_weight, counts, blocks)
    terms = lax.all_to_all(copies, "tm", 0, 0)
    nll = jnp.sum(terms.astype(F32), axis=0).reshape(-1) * (1.0 / (bins * blocks))
    return (latent, nll)


def solution(mesh):
    ring = mesh.shape["neuron"]
    quads = Mesh(mesh.devices.reshape(ring // 4, 4, -1), ("far", "near", "tm"))
    neuron = ("far", "near")
    return jax.shard_map(
        body,
        mesh=quads,
        in_specs=(
            P(neuron, "tm"),
            P(neuron, None),
            P(None, neuron),
            P(neuron),
            P("tm"),
            P(neuron, None),
            P(neuron, None),
        ),
        out_specs=(P("tm", None), P(neuron)),
        check_vma=False,
    )
```

```python
import jax
import jax.numpy as jnp
from jax import lax
from jax.experimental import pallas as pl
from jax.experimental.pallas import tpu as pltpu
from jax.sharding import Mesh
from jax.sharding import PartitionSpec as P

F32 = jnp.float32
BF16 = jnp.bfloat16
ROWS = (((1,), (1,)), ((), ()))
COLUMNS = (((0,), (0,)), ((), ()))
LANES = 128
ROOM = 14 * 1024 * 1024
IN_VMEM = pl.BlockSpec(memory_space=pltpu.VMEM)
IN_HBM = pl.BlockSpec(memory_space=pltpu.HBM)
ANYWHERE = pl.BlockSpec(memory_space=pl.ANY)


def far(array):
    return pltpu.with_memory_space_constraint(array, pltpu.HBM)


def near(array):
    return pltpu.with_memory_space_constraint(array, pltpu.VMEM)


def spread(part, axis):
    count = lax.axis_size(axis)
    copies = jnp.broadcast_to(part[None], (count,) + part.shape)
    return lax.all_to_all(copies, axis, 0, 0)


def reduce_rows(parts):
    quarter = jnp.sum(lax.all_to_all(parts, "near", 0, 0).astype(F32), axis=0)
    return jnp.sum(spread(quarter.astype(BF16), "far").astype(F32), axis=0)


def read_kernel(counts_far, weights_far, part, counts, weights, arrived):
    chunks = arrived.shape[1]
    tall = counts.shape[0] // chunks
    copies = []
    for k in range(chunks):
        here = pl.ds(k * tall, tall)
        for away, here_ref, which in ((counts_far, counts, 0), (weights_far, weights, 1)):
            copies.append(pltpu.make_async_copy(away.at[here], here_ref.at[here], arrived.at[which, k]))
            copies[-1].start()
    acc = None
    for k in range(chunks):
        here = slice(k * tall, (k + 1) * tall)
        copies[2 * k].wait()
        copies[2 * k + 1].wait()
        rows = counts[here, :].astype(F32).astype(BF16)
        one = lax.dot_general(rows, weights[here, :], COLUMNS, preferred_element_type=F32)
        acc = one if acc is None else acc + one
    part[...] = acc.astype(BF16).reshape(part.shape)


def read_in(spikes, read_weight, ring):
    neurons, bins = spikes.shape
    channels = read_weight.shape[1]
    return pl.pallas_call(
        read_kernel,
        in_specs=[IN_HBM, IN_HBM],
        out_specs=IN_VMEM,
        out_shape=jax.ShapeDtypeStruct((ring, bins // ring, channels), BF16),
        scratch_shapes=[
            pltpu.VMEM((neurons, bins), spikes.dtype),
            pltpu.VMEM((neurons, channels), BF16),
            pltpu.SemaphoreType.DMA((2, 8)),
        ],
        compiler_params=pltpu.CompilerParams(vmem_limit_bytes=ROOM),
        name="read_in",
    )(far(spikes), far(read_weight))


def narrow_kernel(counts_far, after, narrow, counts, arrived):
    chunks = arrived.shape[0]
    tall = counts.shape[0] // chunks
    coming = []
    for k in range(chunks):
        here = pl.ds(k * tall, tall)
        coming.append(pltpu.make_async_copy(counts_far.at[here], counts.at[here], arrived.at[k]))
        coming[-1].start()
    for k in range(chunks):
        coming[k].wait()
        here = slice(k * tall, (k + 1) * tall)
        narrow[here, :] = counts[here, :].astype(jnp.int8)


def narrowed(spikes, after):
    return pl.pallas_call(
        narrow_kernel,
        in_specs=[IN_HBM, ANYWHERE],
        out_specs=IN_VMEM,
        out_shape=pltpu.VMEM(spikes.shape, jnp.int8),
        scratch_shapes=[
            pltpu.VMEM(spikes.shape, spikes.dtype),
            pltpu.SemaphoreType.DMA((8,)),
        ],
        compiler_params=pltpu.CompilerParams(vmem_limit_bytes=ROOM),
        name="narrow",
    )(far(spikes), after)


def likelihood_kernel(latent, weights, counts, copies, out_latent, sums):
    wide = 4 * LANES
    rows = latent[...]
    out_latent[...] = rows
    for k in range(weights.shape[0] // wide):
        here = slice(k * wide, (k + 1) * wide)
        log_rate = lax.dot_general(weights[here, :], rows, ROWS, preferred_element_type=F32)
        terms = jnp.exp(log_rate) - counts[here, :].astype(F32) * log_rate
        folded = sum(terms[:, j : j + LANES] for j in range(0, rows.shape[0], LANES))
        for j in range(4):
            turned = folded[j * LANES : (j + 1) * LANES, :].T
            sums[4 * k + j : 4 * k + j + 1, :] = jnp.sum(turned, axis=0, keepdims=True)
    small = sums[...].astype(BF16)
    copies[...] = jnp.broadcast_to(small[None], copies.shape)


def likelihood(latent, read_weight, spikes, blocks):
    neurons = read_weight.shape[0]
    return pl.pallas_call(
        likelihood_kernel,
        in_specs=[IN_VMEM, IN_VMEM, IN_VMEM],
        out_specs=[IN_VMEM, IN_VMEM],
        out_shape=[
            jax.ShapeDtypeStruct((blocks, neurons // LANES, LANES), BF16),
            jax.ShapeDtypeStruct(latent.shape, BF16),
        ],
        scratch_shapes=[pltpu.VMEM((neurons // LANES, LANES), F32)],
        compiler_params=pltpu.CompilerParams(vmem_limit_bytes=ROOM),
        name="likelihood",
    )(near(latent), near(read_weight), near(spikes))


def body(spikes, read_weight, in_proj, decay_rate, gate, out_fwd, out_bwd):
    bins = spikes.shape[1]
    quad = lax.axis_size("near")
    blocks = lax.axis_size("tm")
    place = lax.axis_index("tm")
    log_gate = jnp.log(gate)
    row = lax.broadcasted_iota(jnp.int32, (bins, bins), 0)
    col = lax.broadcasted_iota(jnp.int32, (bins, bins), 1)
    upto = jnp.sum(jnp.where(col <= row, log_gate[None, :], 0.0), axis=1, keepdims=True)
    before = upto - log_gate[:, None]
    upto_t = jnp.sum(jnp.where(row <= col, log_gate[:, None], 0.0), axis=0, keepdims=True)
    before_t = upto_t - log_gate[None, :]
    mix_fwd = jnp.where(col <= row, jnp.exp(jnp.minimum(upto - upto_t, 0.0)), 0.0).astype(BF16)
    mix_bwd = jnp.where(col >= row, jnp.exp(jnp.minimum(before_t - before, 0.0)), 0.0).astype(BF16)
    whole = upto[bins - 1, 0]
    first = lax.broadcasted_iota(jnp.int32, (bins, 1), 0).astype(F32)
    rate = decay_rate[None, :]
    scale_in = jnp.sqrt(-jnp.expm1(-2.0 * rate))
    carry_fwd = jnp.exp((whole - upto) - (bins - 1 - first) * rate) * scale_in
    carry_bwd = jnp.exp(before - first * rate) * scale_in
    cum_fwd = jnp.exp(upto - (first + 1.0) * rate)
    cum_bwd = jnp.exp((whole - before) - (bins - first) * rate)
    grow = jnp.exp((first - bins // 2) * rate)
    shrink = jnp.exp((bins // 2 - first) * rate)

    rows = reduce_rows(read_in(spikes, read_weight, quad))
    power = jnp.mean(rows * rows, axis=-1, keepdims=True) + 1e-05
    normed_rows = (rows * lax.rsqrt(power)).astype(BF16)
    normed = spread(normed_rows, "near").reshape(bins, -1)

    drive = jnp.dot(normed, in_proj, preferred_element_type=F32)
    sent = jnp.stack(
        [
            jnp.sum(drive * carry_fwd, axis=0),
            jnp.sum(drive * carry_bwd, axis=0),
            jnp.broadcast_to(whole, decay_rate.shape),
        ]
    )
    got = spread(sent, "tm")
    drive = drive * scale_in
    state_fwd = jnp.dot(mix_fwd, (drive * grow).astype(BF16), preferred_element_type=F32) * shrink
    state_bwd = jnp.dot(mix_bwd, (drive * shrink).astype(BF16), preferred_element_type=F32) * grow

    loss = got[:, 2, :]
    order = jnp.arange(blocks, dtype=jnp.int32)[:, None]
    earlier = (order >= order.T).astype(F32)
    span = jnp.sum(earlier[:, :, None] * loss[None, :, :], axis=1)
    span_before = span - loss
    at_fwd = jnp.sum(jnp.where(order == place, span_before, 0.0), axis=0)
    at_bwd = jnp.sum(jnp.where(order == place, span, 0.0), axis=0)
    gap_fwd = ((place - 1 - order) * bins).astype(F32) * rate
    gap_bwd = ((order - 1 - place) * bins).astype(F32) * rate
    weight_fwd = jnp.where(order < place, jnp.exp(jnp.minimum(at_fwd[None, :] - span - gap_fwd, 0.0)), 0.0)
    weight_bwd = jnp.where(order > place, jnp.exp(jnp.minimum(span_before - at_bwd[None, :] - gap_bwd, 0.0)), 0.0)
    enter_fwd = jnp.sum(weight_fwd * got[:, 0, :], axis=0)
    enter_bwd = jnp.sum(weight_bwd * got[:, 1, :], axis=0)
    forward = (state_fwd + cum_fwd * enter_fwd[None, :]).astype(BF16)
    backward = (state_bwd + cum_bwd * enter_bwd[None, :]).astype(BF16)
    mixed = jnp.dot(forward, out_fwd, preferred_element_type=F32)
    mixed = mixed + jnp.dot(backward, out_bwd, preferred_element_type=F32)
    mixed_rows = reduce_rows(mixed.astype(BF16).reshape(quad, bins // quad, -1))
    latent_rows = (normed_rows.astype(F32) + mixed_rows).astype(BF16)
    latent = spread(latent_rows, "near").reshape(bins, -1)

    counts = narrowed(spikes, normed_rows)
    copies, latent = likelihood(latent, read_weight, counts, blocks)
    terms = lax.all_to_all(copies, "tm", 0, 0)
    nll = jnp.sum(terms.astype(F32), axis=0).reshape(-1) * (1.0 / (bins * blocks))
    return (latent, nll)


def solution(mesh):
    ring = mesh.shape["neuron"]
    quads = Mesh(mesh.devices.reshape(ring // 4, 4, -1), ("far", "near", "tm"))
    neuron = ("far", "near")
    return jax.shard_map(
        body,
        mesh=quads,
        in_specs=(
            P(neuron, "tm"),
            P(neuron, None),
            P(None, neuron),
            P(neuron),
            P("tm"),
            P(neuron, None),
            P(neuron, None),
        ),
        out_specs=(P("tm", None), P(neuron)),
        check_vma=False,
    )
```

```python
import jax
import jax.numpy as jnp
from jax import lax
from jax.experimental import pallas as pl
from jax.experimental.pallas import tpu as pltpu
from jax.sharding import Mesh
from jax.sharding import PartitionSpec as P

F32 = jnp.float32
BF16 = jnp.bfloat16
ROWS = (((1,), (1,)), ((), ()))
COLUMNS = (((0,), (0,)), ((), ()))
LANES = 128
ROOM = 14 * 1024 * 1024
IN_VMEM = pl.BlockSpec(memory_space=pltpu.VMEM)
IN_HBM = pl.BlockSpec(memory_space=pltpu.HBM)
ANYWHERE = pl.BlockSpec(memory_space=pl.ANY)


def far(array):
    return pltpu.with_memory_space_constraint(array, pltpu.HBM)


def near(array):
    return pltpu.with_memory_space_constraint(array, pltpu.VMEM)


def spread(part, axis):
    count = lax.axis_size(axis)
    copies = jnp.broadcast_to(part[None], (count,) + part.shape)
    return lax.all_to_all(copies, axis, 0, 0)


def reduce_near(parts):
    return jnp.sum(lax.all_to_all(parts, "near", 0, 0).astype(F32), axis=0).astype(BF16)


def reduce_rows(parts):
    return jnp.sum(spread(reduce_near(parts), "far").astype(F32), axis=0)


def read_kernel(counts_far, weights_far, part, counts, weights, arrived):
    chunks = arrived.shape[1]
    tall = counts.shape[0] // chunks
    copies = []
    for k in range(chunks):
        here = pl.ds(k * tall, tall)
        for away, here_ref, which in ((counts_far, counts, 0), (weights_far, weights, 1)):
            copies.append(pltpu.make_async_copy(away.at[here], here_ref.at[here], arrived.at[which, k]))
            copies[-1].start()
    acc = None
    for k in range(chunks):
        here = slice(k * tall, (k + 1) * tall)
        copies[2 * k].wait()
        copies[2 * k + 1].wait()
        rows = counts[here, :].astype(F32).astype(BF16)
        one = lax.dot_general(rows, weights[here, :], COLUMNS, preferred_element_type=F32)
        acc = one if acc is None else acc + one
    part[...] = acc.astype(BF16).reshape(part.shape)


def read_in(spikes, read_weight, ring):
    neurons, bins = spikes.shape
    channels = read_weight.shape[1]
    return pl.pallas_call(
        read_kernel,
        in_specs=[IN_HBM, IN_HBM],
        out_specs=IN_VMEM,
        out_shape=jax.ShapeDtypeStruct((ring, bins // ring, channels), BF16),
        scratch_shapes=[
            pltpu.VMEM((neurons, bins), spikes.dtype),
            pltpu.VMEM((neurons, channels), BF16),
            pltpu.SemaphoreType.DMA((2, 8)),
        ],
        compiler_params=pltpu.CompilerParams(vmem_limit_bytes=ROOM),
        name="read_in",
    )(far(spikes), far(read_weight))


def narrow_kernel(counts_far, after, narrow, counts, arrived):
    chunks = arrived.shape[0]
    tall = counts.shape[0] // chunks
    coming = []
    for k in range(chunks):
        here = pl.ds(k * tall, tall)
        coming.append(pltpu.make_async_copy(counts_far.at[here], counts.at[here], arrived.at[k]))
        coming[-1].start()
    for k in range(chunks):
        coming[k].wait()
        here = slice(k * tall, (k + 1) * tall)
        narrow[here, :] = counts[here, :].astype(jnp.int8)


def narrowed(spikes, after):
    return pl.pallas_call(
        narrow_kernel,
        in_specs=[IN_HBM, ANYWHERE],
        out_specs=IN_VMEM,
        out_shape=pltpu.VMEM(spikes.shape, jnp.int8),
        scratch_shapes=[
            pltpu.VMEM(spikes.shape, spikes.dtype),
            pltpu.SemaphoreType.DMA((8,)),
        ],
        compiler_params=pltpu.CompilerParams(vmem_limit_bytes=ROOM),
        name="narrow",
    )(far(spikes), after)


def likelihood_kernel(latent, weights, counts, copies, out_latent, sums):
    wide = 4 * LANES
    rows = latent[...]
    out_latent[...] = rows
    for k in range(weights.shape[0] // wide):
        here = slice(k * wide, (k + 1) * wide)
        log_rate = lax.dot_general(weights[here, :], rows, ROWS, preferred_element_type=F32)
        terms = jnp.exp(log_rate) - counts[here, :].astype(F32) * log_rate
        folded = sum(terms[:, j : j + LANES] for j in range(0, rows.shape[0], LANES))
        for j in range(4):
            turned = folded[j * LANES : (j + 1) * LANES, :].T
            sums[4 * k + j : 4 * k + j + 1, :] = jnp.sum(turned, axis=0, keepdims=True)
    small = sums[...].astype(BF16)
    copies[...] = jnp.broadcast_to(small[None], copies.shape)


def likelihood(latent, read_weight, spikes, blocks):
    neurons = read_weight.shape[0]
    return pl.pallas_call(
        likelihood_kernel,
        in_specs=[IN_VMEM, IN_VMEM, IN_VMEM],
        out_specs=[IN_VMEM, IN_VMEM],
        out_shape=[
            jax.ShapeDtypeStruct((blocks, neurons // LANES, LANES), BF16),
            jax.ShapeDtypeStruct(latent.shape, BF16),
        ],
        scratch_shapes=[pltpu.VMEM((neurons // LANES, LANES), F32)],
        compiler_params=pltpu.CompilerParams(vmem_limit_bytes=ROOM),
        name="likelihood",
    )(near(latent), near(read_weight), near(spikes))


def tables_of(gate, decay_rate, bin_down, bin_across, order, place):
    bins = gate.shape[0]
    across = jnp.log(gate)[None, :]
    down = jnp.log(gate)[:, None]
    upto = jnp.sum(jnp.where(bin_across <= bin_down, across, 0.0), axis=1, keepdims=True)
    upto_t = jnp.sum(jnp.where(bin_down <= bin_across, down, 0.0), axis=0, keepdims=True)
    whole = jnp.sum(across, axis=1, keepdims=True)
    before = upto - down
    rate = decay_rate[None, :]
    return dict(
        upto=upto,
        upto_t=upto_t,
        before=before,
        before_t=upto_t - across,
        after_upto=whole - upto,
        after_before=whole - before,
        whole=jnp.broadcast_to(whole, rate.shape),
        rate=rate,
        scale=jnp.sqrt(-jnp.expm1(-2.0 * rate)),
        bin_down=bin_down,
        bin_across=bin_across,
        to_last=bins - 1 - bin_down,
        from_start=bin_down + 1.0,
        to_end=bins - bin_down,
        from_half=bin_down - bins // 2,
        to_half=bins // 2 - bin_down,
        earlier=(order >= order.T).astype(F32),
        is_before=(order < place).astype(F32),
        is_here=(order == place).astype(F32),
        is_after=(order > place).astype(F32),
        gap_fwd=(place - 1.0 - order) * bins,
        gap_bwd=(order - 1.0 - place) * bins,
    )


def body(spikes, read_weight, in_proj, decay_rate, gate, out_fwd, out_bwd):
    bins = spikes.shape[1]
    quad = lax.axis_size("near")
    blocks = lax.axis_size("tm")
    bin_down = jnp.arange(bins, dtype=jnp.int32).astype(F32)[:, None]
    bin_across = jnp.arange(bins, dtype=jnp.int32).astype(F32)[None, :]
    order = jnp.arange(blocks, dtype=jnp.int32).astype(F32)[:, None]
    place = lax.axis_index("tm").astype(F32)

    quarter = reduce_near(read_in(spikes, read_weight, quad))
    got, tables = lax.optimization_barrier(
        (spread(quarter, "far"), tables_of(gate, decay_rate, bin_down, bin_across, order, place))
    )
    rows = jnp.sum(got.astype(F32), axis=0)
    power = jnp.mean(rows * rows, axis=-1, keepdims=True) + 1e-05
    normed_rows = (rows * lax.rsqrt(power)).astype(BF16)
    normed = spread(normed_rows, "near").reshape(bins, -1)

    rate, scale = tables["rate"], tables["scale"]
    bin_down, bin_across = tables["bin_down"], tables["bin_across"]
    carry_fwd = jnp.exp(tables["after_upto"] - tables["to_last"] * rate) * scale
    carry_bwd = jnp.exp(tables["before"] - bin_down * rate) * scale
    drive = jnp.dot(normed, in_proj, preferred_element_type=F32)
    sent = jnp.stack(
        [
            jnp.sum(drive * carry_fwd, axis=0),
            jnp.sum(drive * carry_bwd, axis=0),
            tables["whole"][0],
        ]
    )
    got = spread(sent, "tm")

    cum_fwd = jnp.exp(tables["upto"] - tables["from_start"] * rate)
    cum_bwd = jnp.exp(tables["after_before"] - tables["to_end"] * rate)
    grow = jnp.exp(tables["from_half"] * rate)
    shrink = jnp.exp(tables["to_half"] * rate)
    mix_fwd = jnp.where(
        bin_across <= bin_down, jnp.exp(jnp.minimum(tables["upto"] - tables["upto_t"], 0.0)), 0.0
    ).astype(BF16)
    mix_bwd = jnp.where(
        bin_across >= bin_down, jnp.exp(jnp.minimum(tables["before_t"] - tables["before"], 0.0)), 0.0
    ).astype(BF16)
    drive = drive * scale
    state_fwd = jnp.dot(mix_fwd, (drive * grow).astype(BF16), preferred_element_type=F32) * shrink
    state_bwd = jnp.dot(mix_bwd, (drive * shrink).astype(BF16), preferred_element_type=F32) * grow

    loss = got[:, 2, :]
    span = jnp.sum(tables["earlier"][:, :, None] * loss[None, :, :], axis=1)
    span_before = span - loss
    at_fwd = jnp.sum(tables["is_here"] * span_before, axis=0, keepdims=True)
    at_bwd = jnp.sum(tables["is_here"] * span, axis=0, keepdims=True)
    weight_fwd = tables["is_before"] * jnp.exp(jnp.minimum(at_fwd - span - tables["gap_fwd"] * rate, 0.0))
    weight_bwd = tables["is_after"] * jnp.exp(jnp.minimum(span_before - at_bwd - tables["gap_bwd"] * rate, 0.0))
    enter_fwd = jnp.sum(weight_fwd * got[:, 0, :], axis=0)
    enter_bwd = jnp.sum(weight_bwd * got[:, 1, :], axis=0)
    forward = (state_fwd + cum_fwd * enter_fwd[None, :]).astype(BF16)
    backward = (state_bwd + cum_bwd * enter_bwd[None, :]).astype(BF16)
    mixed = jnp.dot(forward, out_fwd, preferred_element_type=F32)
    mixed = mixed + jnp.dot(backward, out_bwd, preferred_element_type=F32)
    mixed_rows = reduce_rows(mixed.astype(BF16).reshape(quad, bins // quad, -1))
    latent_rows = (normed_rows.astype(F32) + mixed_rows).astype(BF16)
    latent = spread(latent_rows, "near").reshape(bins, -1)

    counts = narrowed(spikes, normed_rows)
    copies, latent = likelihood(latent, read_weight, counts, blocks)
    terms = lax.all_to_all(copies, "tm", 0, 0)
    nll = jnp.sum(terms.astype(F32), axis=0).reshape(-1) * (1.0 / (bins * blocks))
    return (latent, nll)


def solution(mesh):
    ring = mesh.shape["neuron"]
    quads = Mesh(mesh.devices.reshape(ring // 4, 4, -1), ("far", "near", "tm"))
    neuron = ("far", "near")
    return jax.shard_map(
        body,
        mesh=quads,
        in_specs=(
            P(neuron, "tm"),
            P(neuron, None),
            P(None, neuron),
            P(neuron),
            P("tm"),
            P(neuron, None),
            P(neuron, None),
        ),
        out_specs=(P("tm", None), P(neuron)),
        check_vma=False,
    )
```

```python
import jax
import jax.numpy as jnp
from jax import lax
from jax.experimental import pallas as pl
from jax.experimental.pallas import tpu as pltpu
from jax.sharding import Mesh
from jax.sharding import PartitionSpec as P

F32 = jnp.float32
BF16 = jnp.bfloat16
ROWS = (((1,), (1,)), ((), ()))
COLUMNS = (((0,), (0,)), ((), ()))
LANES = 128
ROOM = 14 * 1024 * 1024
IN_VMEM = pl.BlockSpec(memory_space=pltpu.VMEM)
IN_HBM = pl.BlockSpec(memory_space=pltpu.HBM)
ANYWHERE = pl.BlockSpec(memory_space=pl.ANY)


def far(array):
    return pltpu.with_memory_space_constraint(array, pltpu.HBM)


def near(array):
    return pltpu.with_memory_space_constraint(array, pltpu.VMEM)


def spread(part, axis):
    count = lax.axis_size(axis)
    copies = jnp.broadcast_to(part[None], (count,) + part.shape)
    return lax.all_to_all(copies, axis, 0, 0)


def sum_quads(parts):
    quarter = jnp.sum(parts.astype(F32), axis=0).astype(BF16)
    return jnp.sum(spread(quarter, "far").astype(F32), axis=0)


def read_kernel(counts_far, weights_far, part, counts, weights, arrived):
    chunks = arrived.shape[1]
    tall = counts.shape[0] // chunks
    copies = []
    for k in range(chunks):
        here = pl.ds(k * tall, tall)
        for away, here_ref, which in ((counts_far, counts, 0), (weights_far, weights, 1)):
            copies.append(pltpu.make_async_copy(away.at[here], here_ref.at[here], arrived.at[which, k]))
            copies[-1].start()
    acc = None
    for k in range(chunks):
        here = slice(k * tall, (k + 1) * tall)
        copies[2 * k].wait()
        copies[2 * k + 1].wait()
        rows = counts[here, :].astype(F32).astype(BF16)
        one = lax.dot_general(rows, weights[here, :], COLUMNS, preferred_element_type=F32)
        acc = one if acc is None else acc + one
    part[...] = acc.astype(BF16).reshape(part.shape)


def read_in(spikes, read_weight, ring):
    neurons, bins = spikes.shape
    channels = read_weight.shape[1]
    return pl.pallas_call(
        read_kernel,
        in_specs=[IN_HBM, IN_HBM],
        out_specs=IN_VMEM,
        out_shape=jax.ShapeDtypeStruct((ring, bins // ring, channels), BF16),
        scratch_shapes=[
            pltpu.VMEM((neurons, bins), spikes.dtype),
            pltpu.VMEM((neurons, channels), BF16),
            pltpu.SemaphoreType.DMA((2, 8)),
        ],
        compiler_params=pltpu.CompilerParams(vmem_limit_bytes=ROOM),
        name="read_in",
    )(far(spikes), far(read_weight))


def narrow_kernel(counts_far, after, narrow, counts, arrived):
    chunks = arrived.shape[0]
    tall = counts.shape[0] // chunks
    coming = []
    for k in range(chunks):
        here = pl.ds(k * tall, tall)
        coming.append(pltpu.make_async_copy(counts_far.at[here], counts.at[here], arrived.at[k]))
        coming[-1].start()
    for k in range(chunks):
        coming[k].wait()
        here = slice(k * tall, (k + 1) * tall)
        narrow[here, :] = counts[here, :].astype(jnp.int8)


def narrowed(spikes, after):
    return pl.pallas_call(
        narrow_kernel,
        in_specs=[IN_HBM, ANYWHERE],
        out_specs=IN_VMEM,
        out_shape=pltpu.VMEM(spikes.shape, jnp.int8),
        scratch_shapes=[
            pltpu.VMEM(spikes.shape, spikes.dtype),
            pltpu.SemaphoreType.DMA((8,)),
        ],
        compiler_params=pltpu.CompilerParams(vmem_limit_bytes=ROOM),
        name="narrow",
    )(far(spikes), after)


def likelihood_kernel(latent, weights, counts, copies, out_latent, sums):
    wide = 4 * LANES
    rows = latent[...]
    out_latent[...] = rows
    for k in range(weights.shape[0] // wide):
        here = slice(k * wide, (k + 1) * wide)
        log_rate = lax.dot_general(weights[here, :], rows, ROWS, preferred_element_type=F32)
        terms = jnp.exp(log_rate) - counts[here, :].astype(F32) * log_rate
        folded = sum(terms[:, j : j + LANES] for j in range(0, rows.shape[0], LANES))
        for j in range(4):
            turned = folded[j * LANES : (j + 1) * LANES, :].T
            sums[4 * k + j : 4 * k + j + 1, :] = jnp.sum(turned, axis=0, keepdims=True)
    small = sums[...].astype(BF16)
    copies[...] = jnp.broadcast_to(small[None], copies.shape)


def likelihood(latent, read_weight, spikes, blocks):
    neurons = read_weight.shape[0]
    return pl.pallas_call(
        likelihood_kernel,
        in_specs=[IN_VMEM, IN_VMEM, IN_VMEM],
        out_specs=[IN_VMEM, IN_VMEM],
        out_shape=[
            jax.ShapeDtypeStruct((blocks, neurons // LANES, LANES), BF16),
            jax.ShapeDtypeStruct(latent.shape, BF16),
        ],
        scratch_shapes=[pltpu.VMEM((neurons // LANES, LANES), F32)],
        compiler_params=pltpu.CompilerParams(vmem_limit_bytes=ROOM),
        name="likelihood",
    )(near(latent), near(read_weight), near(spikes))


def tables_of(gate, decay_rate, bin_down, bin_across, order, place):
    bins = gate.shape[0]
    across = jnp.log(gate)[None, :]
    down = jnp.log(gate)[:, None]
    upto = jnp.sum(jnp.where(bin_across <= bin_down, across, 0.0), axis=1, keepdims=True)
    upto_t = jnp.sum(jnp.where(bin_down <= bin_across, down, 0.0), axis=0, keepdims=True)
    lane = lax.broadcasted_iota(jnp.int32, (1, decay_rate.shape[0]), 1).astype(F32)
    whole = jnp.sum(jnp.where(bin_across >= -bin_down, across, 0.0), axis=1, keepdims=True)
    whole_row = jnp.sum(jnp.where(bin_down >= -lane, down, 0.0), axis=0, keepdims=True)
    before = upto - down
    rate = decay_rate[None, :]
    return dict(
        upto=upto,
        upto_t=upto_t,
        before=before,
        before_t=upto_t - across,
        after_upto=whole - upto,
        after_before=whole - before,
        whole=whole_row,
        rate=rate,
        scale=jnp.sqrt(-jnp.expm1(-2.0 * rate)),
        bin_down=bin_down,
        bin_across=bin_across,
        to_last=bins - 1 - bin_down,
        from_start=bin_down + 1.0,
        to_end=bins - bin_down,
        from_half=bin_down - bins // 2,
        to_half=bins // 2 - bin_down,
        earlier=(order >= order.T).astype(F32),
        is_before=(order < place).astype(F32),
        is_here=(order == place).astype(F32),
        is_after=(order > place).astype(F32),
        gap_fwd=(place - 1.0 - order) * bins,
        gap_bwd=(order - 1.0 - place) * bins,
    )


def body(spikes, read_weight, in_proj, decay_rate, gate, out_fwd, out_bwd):
    bins = spikes.shape[1]
    quad = lax.axis_size("near")
    blocks = lax.axis_size("tm")
    bin_down = jnp.arange(bins, dtype=jnp.int32).astype(F32)[:, None]
    bin_across = jnp.arange(bins, dtype=jnp.int32).astype(F32)[None, :]
    order = jnp.arange(blocks, dtype=jnp.int32).astype(F32)[:, None]
    place = lax.axis_index("tm").astype(F32)

    parts = read_in(spikes, read_weight, quad)
    parts, tables = lax.optimization_barrier(
        (lax.all_to_all(parts, "near", 0, 0), tables_of(gate, decay_rate, bin_down, bin_across, order, place))
    )
    rows = sum_quads(parts)
    power = jnp.mean(rows * rows, axis=-1, keepdims=True) + 1e-05
    normed_rows = (rows * lax.rsqrt(power)).astype(BF16)
    normed = spread(normed_rows, "near").reshape(bins, -1)

    rate, scale = tables["rate"], tables["scale"]
    bin_down, bin_across = tables["bin_down"], tables["bin_across"]
    carry_fwd = jnp.exp(tables["after_upto"] - tables["to_last"] * rate) * scale
    carry_bwd = jnp.exp(tables["before"] - bin_down * rate) * scale
    drive = jnp.dot(normed, in_proj, preferred_element_type=F32)
    sent = jnp.stack(
        [
            jnp.sum(drive * carry_fwd, axis=0),
            jnp.sum(drive * carry_bwd, axis=0),
            tables["whole"][0],
        ]
    )
    got = spread(sent, "tm")

    cum_fwd = jnp.exp(tables["upto"] - tables["from_start"] * rate)
    cum_bwd = jnp.exp(tables["after_before"] - tables["to_end"] * rate)
    grow = jnp.exp(tables["from_half"] * rate)
    shrink = jnp.exp(tables["to_half"] * rate)
    mix_fwd = jnp.where(
        bin_across <= bin_down, jnp.exp(jnp.minimum(tables["upto"] - tables["upto_t"], 0.0)), 0.0
    ).astype(BF16)
    mix_bwd = jnp.where(
        bin_across >= bin_down, jnp.exp(jnp.minimum(tables["before_t"] - tables["before"], 0.0)), 0.0
    ).astype(BF16)
    drive = drive * scale
    state_fwd = jnp.dot(mix_fwd, (drive * grow).astype(BF16), preferred_element_type=F32) * shrink
    state_bwd = jnp.dot(mix_bwd, (drive * shrink).astype(BF16), preferred_element_type=F32) * grow

    loss = got[:, 2, :]
    span = jnp.sum(tables["earlier"][:, :, None] * loss[None, :, :], axis=1)
    span_before = span - loss
    at_fwd = jnp.sum(tables["is_here"] * span_before, axis=0, keepdims=True)
    at_bwd = jnp.sum(tables["is_here"] * span, axis=0, keepdims=True)
    weight_fwd = tables["is_before"] * jnp.exp(jnp.minimum(at_fwd - span - tables["gap_fwd"] * rate, 0.0))
    weight_bwd = tables["is_after"] * jnp.exp(jnp.minimum(span_before - at_bwd - tables["gap_bwd"] * rate, 0.0))
    enter_fwd = jnp.sum(weight_fwd * got[:, 0, :], axis=0)
    enter_bwd = jnp.sum(weight_bwd * got[:, 1, :], axis=0)
    forward = (state_fwd + cum_fwd * enter_fwd[None, :]).astype(BF16)
    backward = (state_bwd + cum_bwd * enter_bwd[None, :]).astype(BF16)
    mixed = jnp.dot(forward, out_fwd, preferred_element_type=F32)
    mixed = mixed + jnp.dot(backward, out_bwd, preferred_element_type=F32)
    parts = mixed.astype(BF16).reshape(quad, bins // quad, -1)
    mixed_rows = sum_quads(lax.all_to_all(parts, "near", 0, 0))
    latent_rows = (normed_rows.astype(F32) + mixed_rows).astype(BF16)
    latent = spread(latent_rows, "near").reshape(bins, -1)

    counts = narrowed(spikes, normed_rows)
    copies, latent = likelihood(latent, read_weight, counts, blocks)
    terms = lax.all_to_all(copies, "tm", 0, 0)
    nll = jnp.sum(terms.astype(F32), axis=0).reshape(-1) * (1.0 / (bins * blocks))
    return (latent, nll)


def solution(mesh):
    ring = mesh.shape["neuron"]
    quads = Mesh(mesh.devices.reshape(ring // 4, 4, -1), ("far", "near", "tm"))
    neuron = ("far", "near")
    return jax.shard_map(
        body,
        mesh=quads,
        in_specs=(
            P(neuron, "tm"),
            P(neuron, None),
            P(None, neuron),
            P(neuron),
            P("tm"),
            P(neuron, None),
            P(neuron, None),
        ),
        out_specs=(P("tm", None), P(neuron)),
        check_vma=False,
    )
```

```python
import jax
import jax.numpy as jnp
from jax import lax
from jax.experimental import pallas as pl
from jax.experimental.pallas import tpu as pltpu
from jax.sharding import Mesh
from jax.sharding import PartitionSpec as P

F32 = jnp.float32
BF16 = jnp.bfloat16
ROWS = (((1,), (1,)), ((), ()))
COLUMNS = (((0,), (0,)), ((), ()))
LANES = 128
ROOM = 14 * 1024 * 1024
IN_VMEM = pl.BlockSpec(memory_space=pltpu.VMEM)
IN_HBM = pl.BlockSpec(memory_space=pltpu.HBM)
ANYWHERE = pl.BlockSpec(memory_space=pl.ANY)


def far(array):
    return pltpu.with_memory_space_constraint(array, pltpu.HBM)


def near(array):
    return pltpu.with_memory_space_constraint(array, pltpu.VMEM)


def spread(part, axis):
    count = lax.axis_size(axis)
    copies = jnp.broadcast_to(part[None], (count,) + part.shape)
    return lax.all_to_all(copies, axis, 0, 0)


def sum_quads(parts):
    quarter = jnp.sum(parts.astype(F32), axis=0).astype(BF16)
    return jnp.sum(spread(quarter, "far").astype(F32), axis=0)


def read_kernel(counts_far, weights_far, part, counts, weights, arrived):
    chunks = arrived.shape[1]
    tall = counts.shape[0] // chunks
    copies = []
    for k in range(chunks):
        here = pl.ds(k * tall, tall)
        for away, here_ref, which in ((counts_far, counts, 0), (weights_far, weights, 1)):
            copies.append(pltpu.make_async_copy(away.at[here], here_ref.at[here], arrived.at[which, k]))
            copies[-1].start()
    acc = None
    for k in range(chunks):
        here = slice(k * tall, (k + 1) * tall)
        copies[2 * k].wait()
        copies[2 * k + 1].wait()
        rows = counts[here, :].astype(F32).astype(BF16)
        one = lax.dot_general(rows, weights[here, :], COLUMNS, preferred_element_type=F32)
        acc = one if acc is None else acc + one
    part[...] = acc.astype(BF16).reshape(part.shape)


def read_in(spikes, read_weight, ring):
    neurons, bins = spikes.shape
    channels = read_weight.shape[1]
    return pl.pallas_call(
        read_kernel,
        in_specs=[IN_HBM, IN_HBM],
        out_specs=IN_VMEM,
        out_shape=jax.ShapeDtypeStruct((ring, bins // ring, channels), BF16),
        scratch_shapes=[
            pltpu.VMEM((neurons, bins), spikes.dtype),
            pltpu.VMEM((neurons, channels), BF16),
            pltpu.SemaphoreType.DMA((2, 8)),
        ],
        compiler_params=pltpu.CompilerParams(vmem_limit_bytes=ROOM),
        name="read_in",
    )(far(spikes), far(read_weight))


def narrow_kernel(counts_far, after, narrow, counts, arrived):
    chunks = arrived.shape[0]
    tall = counts.shape[0] // chunks
    coming = []
    for k in range(chunks):
        here = pl.ds(k * tall, tall)
        coming.append(pltpu.make_async_copy(counts_far.at[here], counts.at[here], arrived.at[k]))
        coming[-1].start()
    for k in range(chunks):
        coming[k].wait()
        here = slice(k * tall, (k + 1) * tall)
        narrow[here, :] = counts[here, :].astype(jnp.int8)


def narrowed(spikes, after):
    return pl.pallas_call(
        narrow_kernel,
        in_specs=[IN_HBM, ANYWHERE],
        out_specs=IN_VMEM,
        out_shape=pltpu.VMEM(spikes.shape, jnp.int8),
        scratch_shapes=[
            pltpu.VMEM(spikes.shape, spikes.dtype),
            pltpu.SemaphoreType.DMA((8,)),
        ],
        compiler_params=pltpu.CompilerParams(vmem_limit_bytes=ROOM),
        name="narrow",
    )(far(spikes), after)


def likelihood_kernel(latent, weights, counts, copies, out_latent, sums, left):
    wide = 4 * LANES
    rows = latent[...]
    leaving = pltpu.make_async_copy(latent, out_latent, left)
    leaving.start()
    for k in range(weights.shape[0] // wide):
        here = slice(k * wide, (k + 1) * wide)
        log_rate = lax.dot_general(weights[here, :], rows, ROWS, preferred_element_type=F32)
        terms = jnp.exp(log_rate) - counts[here, :].astype(F32) * log_rate
        folded = sum(terms[:, j : j + LANES] for j in range(0, rows.shape[0], LANES))
        for j in range(4):
            turned = folded[j * LANES : (j + 1) * LANES, :].T
            sums[4 * k + j : 4 * k + j + 1, :] = jnp.sum(turned, axis=0, keepdims=True)
    small = sums[...].astype(BF16)
    copies[...] = jnp.broadcast_to(small[None], copies.shape)
    leaving.wait()


def likelihood(latent, read_weight, spikes, blocks):
    neurons = read_weight.shape[0]
    return pl.pallas_call(
        likelihood_kernel,
        in_specs=[IN_VMEM, IN_VMEM, IN_VMEM],
        out_specs=[IN_VMEM, IN_HBM],
        out_shape=[
            jax.ShapeDtypeStruct((blocks, neurons // LANES, LANES), BF16),
            pltpu.HBM(latent.shape, BF16),
        ],
        scratch_shapes=[pltpu.VMEM((neurons // LANES, LANES), F32), pltpu.SemaphoreType.DMA],
        compiler_params=pltpu.CompilerParams(vmem_limit_bytes=ROOM),
        name="likelihood",
    )(near(latent), near(read_weight), near(spikes))


def tables_of(gate, decay_rate, bin_down, bin_across, order, place):
    bins = gate.shape[0]
    across = jnp.log(gate)[None, :]
    down = jnp.log(gate)[:, None]
    upto = jnp.sum(jnp.where(bin_across <= bin_down, across, 0.0), axis=1, keepdims=True)
    upto_t = jnp.sum(jnp.where(bin_down <= bin_across, down, 0.0), axis=0, keepdims=True)
    lane = lax.broadcasted_iota(jnp.int32, (1, decay_rate.shape[0]), 1).astype(F32)
    whole = jnp.sum(jnp.where(bin_across >= -bin_down, across, 0.0), axis=1, keepdims=True)
    whole_row = jnp.sum(jnp.where(bin_down >= -lane, down, 0.0), axis=0, keepdims=True)
    before = upto - down
    rate = decay_rate[None, :]
    return dict(
        upto=upto,
        upto_t=upto_t,
        before=before,
        before_t=upto_t - across,
        after_upto=whole - upto,
        after_before=whole - before,
        whole=whole_row,
        rate=rate,
        scale=jnp.sqrt(-jnp.expm1(-2.0 * rate)),
        bin_down=bin_down,
        bin_across=bin_across,
        to_last=bins - 1 - bin_down,
        from_start=bin_down + 1.0,
        to_end=bins - bin_down,
        from_half=bin_down - bins // 2,
        to_half=bins // 2 - bin_down,
        earlier=(order >= order.T).astype(F32),
        is_before=(order < place).astype(F32),
        is_here=(order == place).astype(F32),
        is_after=(order > place).astype(F32),
        gap_fwd=(place - 1.0 - order) * bins,
        gap_bwd=(order - 1.0 - place) * bins,
    )


def body(spikes, read_weight, in_proj, decay_rate, gate, out_fwd, out_bwd):
    bins = spikes.shape[1]
    quad = lax.axis_size("near")
    blocks = lax.axis_size("tm")
    bin_down = jnp.arange(bins, dtype=jnp.int32).astype(F32)[:, None]
    bin_across = jnp.arange(bins, dtype=jnp.int32).astype(F32)[None, :]
    order = jnp.arange(blocks, dtype=jnp.int32).astype(F32)[:, None]
    place = lax.axis_index("tm").astype(F32)

    parts = read_in(spikes, read_weight, quad)
    parts, tables = lax.optimization_barrier(
        (lax.all_to_all(parts, "near", 0, 0), tables_of(gate, decay_rate, bin_down, bin_across, order, place))
    )
    rows = sum_quads(parts)
    power = jnp.mean(rows * rows, axis=-1, keepdims=True) + 1e-05
    normed_rows = (rows * lax.rsqrt(power)).astype(BF16)
    normed = spread(normed_rows, "near").reshape(bins, -1)

    rate, scale = tables["rate"], tables["scale"]
    bin_down, bin_across = tables["bin_down"], tables["bin_across"]
    carry_fwd = jnp.exp(tables["after_upto"] - tables["to_last"] * rate) * scale
    carry_bwd = jnp.exp(tables["before"] - bin_down * rate) * scale
    drive = jnp.dot(normed, in_proj, preferred_element_type=F32)
    sent = jnp.stack(
        [
            jnp.sum(drive * carry_fwd, axis=0),
            jnp.sum(drive * carry_bwd, axis=0),
            tables["whole"][0],
        ]
    )
    got = spread(sent, "tm")

    cum_fwd = jnp.exp(tables["upto"] - tables["from_start"] * rate)
    cum_bwd = jnp.exp(tables["after_before"] - tables["to_end"] * rate)
    grow = jnp.exp(tables["from_half"] * rate)
    shrink = jnp.exp(tables["to_half"] * rate)
    mix_fwd = jnp.where(
        bin_across <= bin_down, jnp.exp(jnp.minimum(tables["upto"] - tables["upto_t"], 0.0)), 0.0
    ).astype(BF16)
    mix_bwd = jnp.where(
        bin_across >= bin_down, jnp.exp(jnp.minimum(tables["before_t"] - tables["before"], 0.0)), 0.0
    ).astype(BF16)
    drive = drive * scale
    state_fwd = jnp.dot(mix_fwd, (drive * grow).astype(BF16), preferred_element_type=F32) * shrink
    state_bwd = jnp.dot(mix_bwd, (drive * shrink).astype(BF16), preferred_element_type=F32) * grow

    loss = got[:, 2, :]
    span = jnp.sum(tables["earlier"][:, :, None] * loss[None, :, :], axis=1)
    span_before = span - loss
    at_fwd = jnp.sum(tables["is_here"] * span_before, axis=0, keepdims=True)
    at_bwd = jnp.sum(tables["is_here"] * span, axis=0, keepdims=True)
    weight_fwd = tables["is_before"] * jnp.exp(jnp.minimum(at_fwd - span - tables["gap_fwd"] * rate, 0.0))
    weight_bwd = tables["is_after"] * jnp.exp(jnp.minimum(span_before - at_bwd - tables["gap_bwd"] * rate, 0.0))
    enter_fwd = jnp.sum(weight_fwd * got[:, 0, :], axis=0)
    enter_bwd = jnp.sum(weight_bwd * got[:, 1, :], axis=0)
    forward = (state_fwd + cum_fwd * enter_fwd[None, :]).astype(BF16)
    backward = (state_bwd + cum_bwd * enter_bwd[None, :]).astype(BF16)
    mixed = jnp.dot(forward, out_fwd, preferred_element_type=F32)
    mixed = mixed + jnp.dot(backward, out_bwd, preferred_element_type=F32)
    parts = mixed.astype(BF16).reshape(quad, bins // quad, -1)
    mixed_rows = sum_quads(lax.all_to_all(parts, "near", 0, 0))
    latent_rows = (normed_rows.astype(F32) + mixed_rows).astype(BF16)
    latent = spread(latent_rows, "near").reshape(bins, -1)

    counts = narrowed(spikes, normed_rows)
    copies, latent = likelihood(latent, read_weight, counts, blocks)
    terms = lax.all_to_all(copies, "tm", 0, 0)
    nll = jnp.sum(terms.astype(F32), axis=0).reshape(-1) * (1.0 / (bins * blocks))
    return (latent, nll)


def solution(mesh):
    ring = mesh.shape["neuron"]
    quads = Mesh(mesh.devices.reshape(ring // 4, 4, -1), ("far", "near", "tm"))
    neuron = ("far", "near")
    return jax.shard_map(
        body,
        mesh=quads,
        in_specs=(
            P(neuron, "tm"),
            P(neuron, None),
            P(None, neuron),
            P(neuron),
            P("tm"),
            P(neuron, None),
            P(neuron, None),
        ),
        out_specs=(P("tm", None), P(neuron)),
        check_vma=False,
    )
```

```python
import jax
import jax.numpy as jnp
from jax import lax
from jax.experimental import pallas as pl
from jax.experimental.pallas import tpu as pltpu
from jax.sharding import Mesh
from jax.sharding import PartitionSpec as P

F32 = jnp.float32
BF16 = jnp.bfloat16
ROWS = (((1,), (1,)), ((), ()))
COLUMNS = (((0,), (0,)), ((), ()))
LANES = 128
ROOM = 14 * 1024 * 1024
IN_VMEM = pl.BlockSpec(memory_space=pltpu.VMEM)
IN_HBM = pl.BlockSpec(memory_space=pltpu.HBM)
ANYWHERE = pl.BlockSpec(memory_space=pl.ANY)


def far(array):
    return pltpu.with_memory_space_constraint(array, pltpu.HBM)


def near(array):
    return pltpu.with_memory_space_constraint(array, pltpu.VMEM)


def spread(part, axis):
    count = lax.axis_size(axis)
    copies = jnp.broadcast_to(part[None], (count,) + part.shape)
    return lax.all_to_all(copies, axis, 0, 0)


def sum_quads(parts):
    quarter = jnp.sum(parts.astype(F32), axis=0).astype(BF16)
    return jnp.sum(spread(quarter, "far").astype(F32), axis=0)


def read_kernel(counts_far, weights_far, part, counts, weights, arrived):
    chunks = arrived.shape[1]
    tall = counts.shape[0] // chunks
    copies = []
    for k in range(chunks):
        here = pl.ds(k * tall, tall)
        for away, here_ref, which in ((counts_far, counts, 0), (weights_far, weights, 1)):
            copies.append(pltpu.make_async_copy(away.at[here], here_ref.at[here], arrived.at[which, k]))
            copies[-1].start()
    acc = None
    for k in range(chunks):
        here = slice(k * tall, (k + 1) * tall)
        copies[2 * k].wait()
        copies[2 * k + 1].wait()
        rows = counts[here, :].astype(F32).astype(BF16)
        one = lax.dot_general(rows, weights[here, :], COLUMNS, preferred_element_type=F32)
        acc = one if acc is None else acc + one
    part[...] = acc.astype(BF16).reshape(part.shape)


def read_in(spikes, read_weight, ring):
    neurons, bins = spikes.shape
    channels = read_weight.shape[1]
    return pl.pallas_call(
        read_kernel,
        in_specs=[IN_HBM, IN_HBM],
        out_specs=IN_VMEM,
        out_shape=jax.ShapeDtypeStruct((ring, bins // ring, channels), BF16),
        scratch_shapes=[
            pltpu.VMEM((neurons, bins), spikes.dtype),
            pltpu.VMEM((neurons, channels), BF16),
            pltpu.SemaphoreType.DMA((2, 4)),
        ],
        compiler_params=pltpu.CompilerParams(vmem_limit_bytes=ROOM),
        name="read_in",
    )(far(spikes), far(read_weight))


def narrow_kernel(counts_far, after, narrow, counts, arrived):
    chunks = arrived.shape[0]
    tall = counts.shape[0] // chunks
    coming = []
    for k in range(chunks):
        here = pl.ds(k * tall, tall)
        coming.append(pltpu.make_async_copy(counts_far.at[here], counts.at[here], arrived.at[k]))
        coming[-1].start()
    for k in range(chunks):
        coming[k].wait()
        here = slice(k * tall, (k + 1) * tall)
        narrow[here, :] = counts[here, :].astype(jnp.int8)


def narrowed(spikes, after):
    return pl.pallas_call(
        narrow_kernel,
        in_specs=[IN_HBM, ANYWHERE],
        out_specs=IN_VMEM,
        out_shape=pltpu.VMEM(spikes.shape, jnp.int8),
        scratch_shapes=[
            pltpu.VMEM(spikes.shape, spikes.dtype),
            pltpu.SemaphoreType.DMA((8,)),
        ],
        compiler_params=pltpu.CompilerParams(vmem_limit_bytes=ROOM),
        name="narrow",
    )(far(spikes), after)


def likelihood_kernel(latent, weights, counts, copies, out_latent, sums, left):
    wide = 4 * LANES
    rows = latent[...]
    leaving = pltpu.make_async_copy(latent, out_latent, left)
    leaving.start()
    for k in range(weights.shape[0] // wide):
        here = slice(k * wide, (k + 1) * wide)
        log_rate = lax.dot_general(weights[here, :], rows, ROWS, preferred_element_type=F32)
        terms = jnp.exp(log_rate) - counts[here, :].astype(F32) * log_rate
        folded = sum(terms[:, j : j + LANES] for j in range(0, rows.shape[0], LANES))
        for j in range(4):
            turned = folded[j * LANES : (j + 1) * LANES, :].T
            sums[4 * k + j : 4 * k + j + 1, :] = jnp.sum(turned, axis=0, keepdims=True)
    small = sums[...].astype(BF16)
    copies[...] = jnp.broadcast_to(small[None], copies.shape)
    leaving.wait()


def likelihood(latent, read_weight, spikes, blocks):
    neurons = read_weight.shape[0]
    return pl.pallas_call(
        likelihood_kernel,
        in_specs=[IN_VMEM, IN_VMEM, IN_VMEM],
        out_specs=[IN_VMEM, IN_HBM],
        out_shape=[
            jax.ShapeDtypeStruct((blocks, neurons // LANES, LANES), BF16),
            pltpu.HBM(latent.shape, BF16),
        ],
        scratch_shapes=[pltpu.VMEM((neurons // LANES, LANES), F32), pltpu.SemaphoreType.DMA],
        compiler_params=pltpu.CompilerParams(vmem_limit_bytes=ROOM),
        name="likelihood",
    )(near(latent), near(read_weight), near(spikes))


def tables_of(gate, decay_rate, bin_down, bin_across, order, place):
    bins = gate.shape[0]
    across = jnp.log(gate)[None, :]
    down = jnp.log(gate)[:, None]
    upto = jnp.sum(jnp.where(bin_across <= bin_down, across, 0.0), axis=1, keepdims=True)
    upto_t = jnp.sum(jnp.where(bin_down <= bin_across, down, 0.0), axis=0, keepdims=True)
    lane = lax.broadcasted_iota(jnp.int32, (1, decay_rate.shape[0]), 1).astype(F32)
    whole = jnp.sum(jnp.where(bin_across >= -bin_down, across, 0.0), axis=1, keepdims=True)
    whole_row = jnp.sum(jnp.where(bin_down >= -lane, down, 0.0), axis=0, keepdims=True)
    before = upto - down
    rate = decay_rate[None, :]
    return dict(
        upto=upto,
        upto_t=upto_t,
        before=before,
        before_t=upto_t - across,
        after_upto=whole - upto,
        after_before=whole - before,
        whole=whole_row,
        rate=rate,
        scale=jnp.sqrt(-jnp.expm1(-2.0 * rate)),
        bin_down=bin_down,
        bin_across=bin_across,
        to_last=bins - 1 - bin_down,
        from_start=bin_down + 1.0,
        to_end=bins - bin_down,
        from_half=bin_down - bins // 2,
        to_half=bins // 2 - bin_down,
        earlier=(order >= order.T).astype(F32),
        is_before=(order < place).astype(F32),
        is_here=(order == place).astype(F32),
        is_after=(order > place).astype(F32),
        gap_fwd=(place - 1.0 - order) * bins,
        gap_bwd=(order - 1.0 - place) * bins,
    )


def body(spikes, read_weight, in_proj, decay_rate, gate, out_fwd, out_bwd):
    bins = spikes.shape[1]
    quad = lax.axis_size("near")
    blocks = lax.axis_size("tm")
    bin_down = jnp.arange(bins, dtype=jnp.int32).astype(F32)[:, None]
    bin_across = jnp.arange(bins, dtype=jnp.int32).astype(F32)[None, :]
    order = jnp.arange(blocks, dtype=jnp.int32).astype(F32)[:, None]
    place = lax.axis_index("tm").astype(F32)

    parts = read_in(spikes, read_weight, quad)
    parts, tables = lax.optimization_barrier(
        (lax.all_to_all(parts, "near", 0, 0), tables_of(gate, decay_rate, bin_down, bin_across, order, place))
    )
    rows = sum_quads(parts)
    power = jnp.mean(rows * rows, axis=-1, keepdims=True) + 1e-05
    normed_rows = (rows * lax.rsqrt(power)).astype(BF16)
    normed = spread(normed_rows, "near").reshape(bins, -1)

    rate, scale = tables["rate"], tables["scale"]
    bin_down, bin_across = tables["bin_down"], tables["bin_across"]
    carry_fwd = jnp.exp(tables["after_upto"] - tables["to_last"] * rate) * scale
    carry_bwd = jnp.exp(tables["before"] - bin_down * rate) * scale
    drive = jnp.dot(normed, in_proj, preferred_element_type=F32)
    sent = jnp.stack(
        [
            jnp.sum(drive * carry_fwd, axis=0),
            jnp.sum(drive * carry_bwd, axis=0),
            tables["whole"][0],
        ]
    )
    got = spread(sent, "tm")

    cum_fwd = jnp.exp(tables["upto"] - tables["from_start"] * rate)
    cum_bwd = jnp.exp(tables["after_before"] - tables["to_end"] * rate)
    grow = jnp.exp(tables["from_half"] * rate)
    shrink = jnp.exp(tables["to_half"] * rate)
    mix_fwd = jnp.where(
        bin_across <= bin_down, jnp.exp(jnp.minimum(tables["upto"] - tables["upto_t"], 0.0)), 0.0
    ).astype(BF16)
    mix_bwd = jnp.where(
        bin_across >= bin_down, jnp.exp(jnp.minimum(tables["before_t"] - tables["before"], 0.0)), 0.0
    ).astype(BF16)
    drive = drive * scale
    state_fwd = jnp.dot(mix_fwd, (drive * grow).astype(BF16), preferred_element_type=F32) * shrink
    state_bwd = jnp.dot(mix_bwd, (drive * shrink).astype(BF16), preferred_element_type=F32) * grow

    loss = got[:, 2, :]
    span = jnp.sum(tables["earlier"][:, :, None] * loss[None, :, :], axis=1)
    span_before = span - loss
    at_fwd = jnp.sum(tables["is_here"] * span_before, axis=0, keepdims=True)
    at_bwd = jnp.sum(tables["is_here"] * span, axis=0, keepdims=True)
    weight_fwd = tables["is_before"] * jnp.exp(jnp.minimum(at_fwd - span - tables["gap_fwd"] * rate, 0.0))
    weight_bwd = tables["is_after"] * jnp.exp(jnp.minimum(span_before - at_bwd - tables["gap_bwd"] * rate, 0.0))
    enter_fwd = jnp.sum(weight_fwd * got[:, 0, :], axis=0)
    enter_bwd = jnp.sum(weight_bwd * got[:, 1, :], axis=0)
    forward = (state_fwd + cum_fwd * enter_fwd[None, :]).astype(BF16)
    backward = (state_bwd + cum_bwd * enter_bwd[None, :]).astype(BF16)
    mixed = jnp.dot(forward, out_fwd, preferred_element_type=F32)
    mixed = mixed + jnp.dot(backward, out_bwd, preferred_element_type=F32)
    parts = mixed.astype(BF16).reshape(quad, bins // quad, -1)
    mixed_rows = sum_quads(lax.all_to_all(parts, "near", 0, 0))
    latent_rows = (normed_rows.astype(F32) + mixed_rows).astype(BF16)
    latent = spread(latent_rows, "near").reshape(bins, -1)

    counts = narrowed(spikes, normed_rows)
    copies, latent = likelihood(latent, read_weight, counts, blocks)
    terms = lax.all_to_all(copies, "tm", 0, 0)
    nll = jnp.sum(terms.astype(F32), axis=0).reshape(-1) * (1.0 / (bins * blocks))
    return (latent, nll)


def solution(mesh):
    ring = mesh.shape["neuron"]
    quads = Mesh(mesh.devices.reshape(ring // 4, 4, -1), ("far", "near", "tm"))
    neuron = ("far", "near")
    return jax.shard_map(
        body,
        mesh=quads,
        in_specs=(
            P(neuron, "tm"),
            P(neuron, None),
            P(None, neuron),
            P(neuron),
            P("tm"),
            P(neuron, None),
            P(neuron, None),
        ),
        out_specs=(P("tm", None), P(neuron)),
        check_vma=False,
    )
```
